256 devices in a mesh: ctx: 64 (over y, z, core), mp: 4 (over x).
Axes of the slice: x: 4, y: 4, z: 8, core: 2. Of those that a mesh axis runs over, the one named last changes fastest.
Arguments:
- query: bfloat16 [256, 8, 8, 128], P(('ctx', 'mp')), may hold values from -8 to 8
- keys: bfloat16 [256, 8, 2048, 128], P(('ctx', 'mp')), may hold values from -5 to 5
- values: bfloat16 [256, 8, 2048, 128], P(('ctx', 'mp')), may hold values from -6 to 6
- chosen: int32 [8, 256, 16], replicated, may hold values from 0 to 255, all different within a row; in each aligned block of 256 rows (0 to 255, 256 to 511, ..., all dimensions but the last counted through in order) at most 64 rows name the same one
- residual: bfloat16 [256, 8192], P('ctx', 'mp'), may hold values from -1.5 to 1.5
- output_weight: bfloat16 [8192, 8192], P('ctx', 'mp'), may hold values from -0.0625 to 0.0625
- norm_gain: float32 [8192], P('mp'), may hold values from 0.5 to 1.5
- gate_weight: bfloat16 [8192, 14336], P('mp', 'ctx'), may hold values from -0.0625 to 0.0625
- up_weight: bfloat16 [8192, 14336], P('mp', 'ctx'), may hold values from -0.0625 to 0.0625
- down_weight: bfloat16 [14336, 8192], P('ctx', 'mp'), may hold values from -0.046875 to 0.046875
Outputs:
- stream: bfloat16 [256, 8192], P('ctx', 'mp')
- update: bfloat16 [256, 8192], P('ctx', 'mp')
The draws below stay inside these ranges and needn't reach their ends.
Inputs may be any that keep to these rules, and one draw needn't show every extreme that they name: `chosen`: for each KV head, each row lists 16 different partitions; no partition is listed by more than 64 rows of one KV head, and in every draw some partition is listed by exactly 64 rows of some KV head.
All inputs are finite; a program needn't handle non-finite values.
Results may differ from the reference program's by a relative error of at most 0.025.
Values may be sent and summed in bfloat16 or wider, within the bound.
A program may use at most 128 MiB of HBM per device.

```python
import math
import jax
import jax.numpy as jnp
import numpy as np
from jax import lax

MODEL_WIDTH = 8192
KEY_HEADS = 8
QUERY_PER_KEY = 8
HEAD_WIDTH = 128
FF = 14336
PARTITION_KEYS = 2048
KEPT_PARTITIONS = 16
DECODED_COUNT = 256
PARTITION_COUNT = 256
ROW_LIMIT = 64


def draw_keys(key, part):
    array_shape = (PARTITION_COUNT, KEY_HEADS, PARTITION_KEYS, HEAD_WIDTH)
    base = jnp.clip(jax.random.normal(jax.random.fold_in(key, 21), array_shape, jnp.float32), -5.0, 5.0)
    return base.astype(jnp.bfloat16)


def draw_query(key, part):
    array_shape = (DECODED_COUNT, KEY_HEADS, QUERY_PER_KEY, HEAD_WIDTH)
    base = jnp.clip(2.7 * jax.random.normal(jax.random.fold_in(key, 31), array_shape, jnp.float32), -8.0, 8.0)
    return base.astype(jnp.bfloat16)


def draw_residual(key, part):
    row_scale = 10.0 ** jax.random.uniform(jax.random.fold_in(key, 41), (DECODED_COUNT, 1), jnp.float32, -0.5, 0.5)
    column_rise = 3.0 ** (jnp.arange(MODEL_WIDTH, dtype=jnp.float32) / MODEL_WIDTH - 0.5)
    column_scale = column_rise * 10.0 ** jax.random.uniform(jax.random.fold_in(key, 42), (MODEL_WIDTH,), jnp.float32, -0.5, 0.5)
    base = jax.random.normal(jax.random.fold_in(key, 43), (DECODED_COUNT, MODEL_WIDTH), jnp.float32)
    return jnp.clip(0.15 * base * row_scale * column_scale[None, :], -1.5, 1.5).astype(jnp.bfloat16)


def block_scale(stream_key, shape, pieces, low, high):
    gain = 1.0
    for dim, blocks in pieces:
        steps = jax.random.uniform(jax.random.fold_in(jax.random.fold_in(stream_key, 6), dim), (blocks,), jnp.float32, low / len(pieces), high / len(pieces))
        gain = gain * jnp.repeat(jnp.exp(steps), shape[dim] // blocks).reshape((-1,) + (1,) * (len(shape) - 1 - dim))
    return gain


def routed_block(key, own, number, rows, number_of, top, reach, skew):
    ranking = jax.random.permutation(key, number_of)
    packed, common = load_shares(number_of, rows * top, reach, skew, True), load_shares(number_of, rows * top, reach, skew, False)
    places = jnp.arange(number_of)

    def named(lengths, turn):
        used = int((lengths > 0).sum())
        fixed = max(1, used // 4)
        shifted = fixed + (places - fixed + turn * (used - fixed)) % max(1, number_of - fixed)
        return jnp.zeros((number_of,), jnp.int32).at[ranking[jnp.where(places < fixed, places, shifted)]].set(jnp.asarray(lengths, jnp.int32))

    lengths = jnp.where(number % 4 == 0, named(packed, number // 4), named(common, number - number // 4 - 1))
    mixed = jax.random.permutation(jax.random.fold_in(own, 3), number_of)
    giver, taker = mixed[0:number_of // 2 * 2:2], mixed[1:number_of // 2 * 2:2]
    room = jnp.minimum(lengths[giver] - 1, reach - lengths[taker]) // 2
    room = jnp.where((giver == ranking[0]) | (taker == ranking[0]) | (lengths[taker] == 0), 0, jnp.maximum(room, 0))
    shifted = jax.random.randint(jax.random.fold_in(own, 4), (number_of // 2,), 0, 1 << 20) % (room + 1)
    lengths = lengths.at[giver].add(-shifted).at[taker].add(shifted)
    members = jnp.searchsorted(jnp.cumsum(lengths), jnp.arange(rows * top), side="right").astype(jnp.int32)
    grid = members.reshape(top, rows).T
    grid = grid[jax.random.permutation(jax.random.fold_in(own, 1), rows)]
    turn = jax.random.randint(jax.random.fold_in(own, 2), (rows, 1), 0, top)
    return jnp.take_along_axis(grid, (jnp.arange(top)[None, :] + turn) % top, axis=1)


def load_shares(count, total, reach, lean, full):
    portions = [(1 << 20) // math.isqrt(rank ** lean) + 1 for rank in range(1, count + 1)]
    largest = reach if full else min(reach, max(-(-total // count), total * portions[0] // sum(portions)))
    least = 1 if total - largest >= count - 1 else 0
    holding, surplus = [largest] + [least] * (count - 1), total - largest - least * (count - 1)
    while surplus > 0:
        free = [i for i in range(1, count) if holding[i] < largest] or [i for i in range(1, count) if holding[i] < reach]
        whole, budget = sum([portions[i] for i in free]), surplus
        for i in free:
            addition = min(reach - holding[i], max(1, budget * portions[i] // whole), surplus)
            holding[i] = holding[i] + addition
            surplus = surplus - addition
    return np.array(holding)


def scatter_about(stream_key, shape, width, reach, shards=(), held_as=jnp.bfloat16):
    array = width * jax.random.normal(stream_key, shape, jnp.float32)
    if shards:
        array = array * block_scale(stream_key, shape, shards, -0.22, 0.18)
    return jnp.clip(array, -reach, reach).astype(held_as)


def setup_inputs(seed: int = 0) -> dict:
    arg_keys = jax.random.split(jax.random.key(seed), 11)
    query = draw_query(jax.random.fold_in(arg_keys[10], 71), 0)
    keys = draw_keys(jax.random.fold_in(arg_keys[10], 71), 0)
    values = scatter_about(arg_keys[2], (PARTITION_COUNT, KEY_HEADS, PARTITION_KEYS, HEAD_WIDTH), 1.0, 6.0, ((0, 256),))
    chosen_keys = jax.random.split(jax.random.fold_in(arg_keys[3], 1), KEY_HEADS * DECODED_COUNT // DECODED_COUNT)
    chosen_turns = jax.random.permutation(jax.random.fold_in(arg_keys[3], 3), KEY_HEADS * DECODED_COUNT // DECODED_COUNT)
    chosen = jax.vmap(lambda own, number: routed_block(jax.random.fold_in(arg_keys[3], 2), own, number, DECODED_COUNT, PARTITION_COUNT, KEPT_PARTITIONS, ROW_LIMIT, 2))(chosen_keys, chosen_turns).reshape((KEY_HEADS, DECODED_COUNT, KEPT_PARTITIONS))
    residual = draw_residual(jax.random.fold_in(arg_keys[10], 71), 0)
    output_weight = scatter_about(arg_keys[5], (KEY_HEADS * QUERY_PER_KEY * HEAD_WIDTH, MODEL_WIDTH), (KEY_HEADS * QUERY_PER_KEY * HEAD_WIDTH) ** -0.5, 0.0625, ((0, 64), (1, 4)))
    norm_gain = jnp.clip(1.0 + 0.1 * jax.random.normal(arg_keys[6], (MODEL_WIDTH,), jnp.float32), 0.5, 1.5)
    gate_weight = scatter_about(arg_keys[7], (MODEL_WIDTH, FF), MODEL_WIDTH ** -0.5, 0.0625, ((0, 4), (1, 64)))
    up_weight = scatter_about(arg_keys[8], (MODEL_WIDTH, FF), MODEL_WIDTH ** -0.5, 0.0625, ((0, 4), (1, 64)))
    down_weight = scatter_about(arg_keys[9], (FF, MODEL_WIDTH), FF ** -0.5, 0.046875, ((0, 64), (1, 4)))
    return {"query": query, "keys": keys, "values": values, "chosen": chosen, "residual": residual, "output_weight": output_weight, "norm_gain": norm_gain, "gate_weight": gate_weight, "up_weight": up_weight, "down_weight": down_weight}


norm_eps = 1e-05

def reference(query, keys, values, chosen, residual, output_weight, norm_gain, gate_weight, up_weight, down_weight):
    head_dim = query.shape[3]
    score_scale = head_dim ** (-0.5)
    head_ids = jnp.arange(keys.shape[1], dtype=jnp.int32)

    def one_row(inputs):
        query_row, listed = inputs
        key_sel = keys[listed, head_ids[:, None]]
        value_sel = values[listed, head_ids[:, None]]
        scores = jnp.einsum('hgd,hkjd->hkgj', query_row.astype(jnp.float32), key_sel.astype(jnp.float32)) * score_scale
        block_max = lax.optimization_barrier(jnp.max(scores, axis=3))
        probs = jnp.exp(scores - block_max[..., None])
        block_sum = lax.optimization_barrier(jnp.sum(probs, axis=3))
        probs_low = lax.optimization_barrier(probs.astype(jnp.bfloat16))
        block_value = jnp.einsum('hkgj,hkjd->hkgd', probs_low.astype(jnp.float32), value_sel.astype(jnp.float32))
        row_top = lax.optimization_barrier(jnp.max(block_max, axis=1))
        factor = jnp.exp(block_max - row_top[:, None, :])
        numerator = lax.optimization_barrier(jnp.sum(factor[..., None] * block_value, axis=1))
        denominator = lax.optimization_barrier(jnp.sum(factor * block_sum, axis=1))
        return (numerator / denominator[..., None]).astype(jnp.bfloat16)
    attended = lax.map(one_row, (query, jnp.transpose(chosen, (1, 0, 2))))
    attended = attended.reshape(query.shape[0], -1)
    projected = jnp.dot(attended, output_weight, preferred_element_type=jnp.float32)
    stream = (residual.astype(jnp.float32) + projected).astype(jnp.bfloat16)
    stream_wide = stream.astype(jnp.float32)
    mean_square = lax.optimization_barrier(jnp.mean(stream_wide * stream_wide, axis=1, keepdims=True))
    normed = (stream_wide * lax.rsqrt(mean_square + norm_eps) * norm_gain).astype(jnp.bfloat16)
    gate = jnp.dot(normed, gate_weight, preferred_element_type=jnp.float32)
    up_part = jnp.dot(normed, up_weight, preferred_element_type=jnp.float32)
    hidden = (jax.nn.silu(gate) * up_part).astype(jnp.bfloat16)
    update = jnp.dot(hidden, down_weight, preferred_element_type=jnp.float32).astype(jnp.bfloat16)
    return (stream, update)
```

```python
import functools
import math

import jax
import jax.numpy as jnp
from jax import lax
from jax.experimental import pallas as pl
from jax.experimental.pallas import tpu as pltpu
from jax.sharding import PartitionSpec as P

NX, NY, NZ, NK = 4, 4, 8, 2
CTX = NY * NZ * NK
ROWS, HEADS, GROUP, WIDTH = 256, 8, 8, 128
KEYS, SLOTS = 2048, 64
MODEL, LOCAL, UNITS = 8192, 2048, 224
MSG = SLOTS + 16
EPS = 1e-5
LOWEST = -1e30
SCALE = WIDTH**-0.5 * math.log2(math.e)
MESH = pl.DeviceIdType.MESH
VMEM_LIMIT = 56 * 1024 * 1024
F32, BF16 = jnp.float32, jnp.bfloat16


def place():
    c = lax.axis_index("ctx")
    x = lax.axis_index("mp")
    return c, x, c // (NZ * NK), (c // NK) % NZ, c % NK


def ctx_of(y, z, k):
    return (y * NZ + z) * NK + k


def remote(src, dst, send_sem, recv_sem, ctx, mp):
    return pltpu.make_async_remote_copy(
        src_ref=src,
        dst_ref=dst,
        send_sem=send_sem,
        recv_sem=recv_sem,
        device_id=(ctx, mp),
        device_id_type=MESH,
    )


def dot(a, b, da, db):
    return lax.dot_general(a, b, (((da,), (db,)), ((), ())), preferred_element_type=F32)


def attend_kernel(
    slots_ref, own_ref, rank_ref, keys_ref, values_ref, out_ref,
    qbuf, kbuf, vbuf, q32, o32, st32, sendbuf,
    k_sem, v_sem,
    z_send, z_recv, p2_send, p2_recv, p3_send, p3_recv, c_send, c_recv,
    a_send, a_recv,
):
    c, x, y, z, k = place()

    barrier = pltpu.get_barrier_semaphore()

    def greet(j, carry):
        @pl.when(j != c)
        def _():
            pl.semaphore_signal(barrier, inc=1, device_id=(j, x), device_id_type=MESH)

        return carry

    lax.fori_loop(0, CTX, greet, 0)
    for j in range(1, NX):
        pl.semaphore_signal(barrier, inc=1, device_id=(c, (x + j) % NX), device_id_type=MESH)

    def load(t, carry):
        h = (c // GROUP + t) % HEADS
        pltpu.make_async_copy(keys_ref.at[h], kbuf.at[h], k_sem.at[h]).start()
        pltpu.make_async_copy(values_ref.at[h], vbuf.at[h], v_sem.at[h]).start()
        return carry

    lax.fori_loop(0, HEADS, load, 0)

    row_a = ((k * NX + x) * NY + y) * NZ
    row_b = ((k * NY + y) * NX + x) * NZ
    qbuf[0:2, row_a + z] = own_ref[0:2]
    qbuf[2:4, row_b + z] = own_ref[2:4]
    pl.semaphore_wait(barrier, CTX - 1 + NX - 1)

    z_copies = []
    for j in range(1, NZ):
        to = ctx_of(y, (z + j) % NZ, k)
        for half, row in ((0, row_a), (1, row_b)):
            ref = qbuf.at[pl.ds(2 * half, 2), row + z]
            cp = remote(ref, ref, z_send.at[half, j - 1], z_recv.at[half, j - 1], to, x)
            cp.start()
            z_copies.append(cp)
    for cp in z_copies:
        cp.wait_recv()

    p2 = []
    for j in range(1, 4):
        ref = qbuf.at[0:2, pl.ds(row_a, NZ)]
        cp = remote(ref, ref, p2_send.at[0, j - 1], p2_recv.at[0, j - 1], ctx_of((y + j) % NY, z, k), x)
        cp.start()
        p2.append(cp)
        ref = qbuf.at[2:4, pl.ds(row_b, NZ)]
        cp = remote(ref, ref, p2_send.at[1, j - 1], p2_recv.at[1, j - 1], c, (x + j) % NX)
        cp.start()
        p2.append(cp)
    for cp in p2:
        cp.wait_recv()

    other = ctx_of(y, z, 1 - k)
    base = {0: k * NX + x, 1: k * NY + y}
    order = (0, 2, 1, 3)
    p3 = {}
    cores = []

    def pass_on(hp, block, n):
        ref = qbuf.at[hp, pl.ds(block * 32, 32)]
        cp = remote(ref, ref, c_send.at[hp, n], c_recv.at[hp, n], other, x)
        cp.start()
        cores.append(cp)

    for hp in order:
        for j in range(1, 4):
            ref = qbuf.at[hp, pl.ds(base[hp // 2] * 32, 32)]
            if hp < 2:
                cp = remote(ref, ref, p3_send.at[hp, j - 1], p3_recv.at[hp, j - 1], c, (x + j) % NX)
            else:
                cp = remote(ref, ref, p3_send.at[hp, j - 1], p3_recv.at[hp, j - 1], ctx_of((y + j) % NY, z, k), x)
            cp.start()
            p3[hp, j] = cp
    for hp in order:
        pass_on(hp, base[hp // 2], 0)
    for hp in order:
        for j in range(1, 4):
            p3[hp, j].wait_recv()
            source = (x - j + NX) % NX if hp < 2 else (y - j + NY) % NY
            pass_on(hp, k * 4 + source, j)
    for cp in cores:
        cp.wait_recv()

    slot_iota = lax.broadcasted_iota(jnp.int32, (SLOTS, ROWS), 0).astype(F32)

    def head(t, carry):
        h = (c // GROUP + t) % HEADS
        hp = h // 2
        upper = (h % 2) == 1
        pltpu.make_async_copy(keys_ref.at[h], kbuf.at[h], k_sem.at[h]).wait()
        pltpu.make_async_copy(values_ref.at[h], vbuf.at[h], v_sem.at[h]).wait()

        def pick(i, carry2):
            for u in range(8):
                s = i * 8 + u
                tile = qbuf[hp, slots_ref[h * SLOTS + s]].astype(F32)
                q32[pl.ds(pl.multiple_of(s * 8, 8), 8), :] = jnp.where(upper, tile[8:16], tile[0:8])
            return carry2

        lax.fori_loop(0, SLOTS // 8, pick, 0)

        for b in range(2):
            at = pl.ds(b * 256, 256)
            s = dot(q32[at, :].astype(BF16), kbuf[h], 1, 1)
            top = (jnp.max(s, axis=1, keepdims=True) * SCALE).astype(BF16).astype(F32)
            p = jnp.exp2(s * SCALE - top)
            total = jnp.sum(p, axis=1, keepdims=True)
            o32[at, :] = dot(p.astype(BF16), vbuf[h], 1, 0)
            lane = lax.broadcasted_iota(jnp.int32, (256, WIDTH), 1)
            st32[at, :] = jnp.where(lane == 0, top, total)

        hit = slot_iota == rank_ref[pl.ds(h, 1), :]
        for g in range(GROUP):
            n = h * GROUP + g
            sendbuf[n, 0:SLOTS, :] = o32[pl.ds(g, SLOTS, stride=GROUP), :].astype(BF16)
            st = st32[pl.ds(g, SLOTS, stride=GROUP), :]
            top = jnp.sum(jnp.where(hit, st[:, 0:1], 0.0), axis=0, keepdims=True)
            total = jnp.sum(jnp.where(hit, st[:, 1:2], 0.0), axis=0, keepdims=True)
            high = total.astype(BF16).astype(F32)
            low = total - high
            tile = jnp.concatenate(
                [
                    top[:, :128], top[:, 128:], high[:, :128], high[:, 128:],
                    low[:, :128], low[:, 128:], jnp.zeros((10, 128), F32),
                ],
                axis=0,
            )
            sendbuf[n, SLOTS:MSG, :] = tile.astype(BF16)

            @pl.when(n != c)
            def _():
                remote(sendbuf.at[n], out_ref.at[c], a_send.at[n], a_recv.at[c], n, x).start()

            @pl.when(n == c)
            def _():
                out_ref[c] = sendbuf[n]

        return carry

    lax.fori_loop(0, HEADS, head, 0)

    for cp in z_copies:
        cp.wait_send()
    for cp in p2:
        cp.wait_send()
    for cp in p3.values():
        cp.wait_send()
    for cp in cores:
        cp.wait_send()

    def finish(j, carry):
        @pl.when(j != c)
        def _():
            cp = remote(sendbuf.at[j], out_ref.at[j], a_send.at[j], a_recv.at[j], j, x)
            cp.wait_recv()
            cp.wait_send()

        return carry

    lax.fori_loop(0, CTX, finish, 0)


def swap4(v):
    return pltpu.roll(v, 4, 1)


def regroup(acc, out_ref):
    parts = [acc[:, b * 512 : (b + 1) * 512].reshape(4, 8, 512) for b in range(4)]
    lower = lax.broadcasted_iota(jnp.int32, (4, 8, 512), 1) < 4
    even = [jnp.where(lower, parts[b], swap4(parts[b + 1])) for b in (0, 2)]
    odd = [jnp.where(lower, swap4(parts[b]), parts[b + 1]) for b in (0, 2)]
    for t in range(4):
        out_ref[2 * t] = jnp.concatenate([even[0][t], even[1][t]], axis=0).astype(BF16)
        out_ref[2 * t + 1] = jnp.concatenate([odd[0][t], odd[1][t]], axis=0).astype(BF16)


def ungroup(src_ref, store):
    a = src_ref[...].astype(F32)
    lower = lax.broadcasted_iota(jnp.int32, (8, 512), 0) < 4
    columns = [[], [], [], []]
    for t in range(4):
        for q in range(2):
            e = a[2 * t, 8 * q : 8 * q + 8]
            o = a[2 * t + 1, 8 * q : 8 * q + 8]
            columns[2 * q].append(jnp.where(lower, e, pltpu.roll(o, 4, 0)))
            columns[2 * q + 1].append(jnp.where(lower, pltpu.roll(e, 4, 0), o))
    for b in range(4):
        store(b, jnp.concatenate(columns[b], axis=0).astype(BF16))


def layer_kernel(
    msg_ref, rank_ref, residual_ref, gain_ref, wo_hbm, wg_hbm, wu_hbm, wd_hbm,
    stream_ref, update_ref,
    wo, wg, wu, wd, weight, stats, weights, num_t, xmsg, att_t,
    core_out, core_in, y_out, y_in, z_out, z_in,
    z_all, x_all, gu32, gu_out, gu_in, hid,
    w_sem, x_send, x_recv,
    c_send, c_recv, y_send, y_recv, z_send, z_recv,
    gz_send, gz_recv, gy_send, gy_recv, gc_send, gc_recv,
    r_send, r_recv, h_send, h_recv,
):
    c, x, y, z, k = place()
    other = ctx_of(y, z, 1 - k)
    barrier = pltpu.get_barrier_semaphore()
    pl.semaphore_signal(barrier, inc=1, device_id=(other, x), device_id_type=MESH)
    for j in range(1, NX):
        pl.semaphore_signal(barrier, inc=1, device_id=(c, (x + j) % NX), device_id_type=MESH)
    for j in range(1, NY):
        pl.semaphore_signal(barrier, inc=1, device_id=(ctx_of((y + j) % NY, z, k), x), device_id_type=MESH)
    for j in range(1, NZ):
        pl.semaphore_signal(barrier, inc=1, device_id=(ctx_of(y, (z + j) % NZ, k), x), device_id_type=MESH)

    loads = [
        pltpu.make_async_copy(wo_hbm, wo, w_sem.at[0]),
        pltpu.make_async_copy(wg_hbm, wg, w_sem.at[1]),
        pltpu.make_async_copy(wu_hbm, wu, w_sem.at[2]),
        pltpu.make_async_copy(wd_hbm, wd.at[pl.ds(0, UNITS)], w_sem.at[3]),
    ]
    for cp in loads:
        cp.start()
    wd[UNITS:256, :] = jnp.zeros((256 - UNITS, LOCAL), BF16)

    def spread(s, carry):
        stats[pl.ds(pl.multiple_of(s * 16, 16), 16), :] = msg_ref[s, SLOTS:MSG, :].astype(F32)
        return carry

    lax.fori_loop(0, CTX, spread, 0)

    def row_of(n):
        return jnp.concatenate([stats[pl.ds(2 * n + i, CTX, stride=16), :] for i in range(2)], axis=1)

    listed = rank_ref[...] >= 0.0
    top_each = jnp.where(listed, row_of(0), LOWEST)
    top = jnp.max(top_each, axis=0, keepdims=True)
    w = jnp.where(listed, jnp.exp2(top_each - top), 0.0).astype(BF16).astype(F32)
    weights[...] = w
    den = jnp.sum(w * (row_of(1) + row_of(2)), axis=0, keepdims=True)

    num_t[...] = jnp.zeros_like(num_t)
    slot_iota = lax.broadcasted_iota(jnp.int32, (SLOTS, ROWS), 0).astype(F32)

    def merge(i, carry):
        for u in range(4):
            s = i * 4 + u
            hit = slot_iota == rank_ref[pl.ds(s, 1), :]
            weight[pl.ds(u * SLOTS, SLOTS), :] = jnp.where(hit, weights[pl.ds(s, 1), :], 0.0).astype(BF16)
        values = jnp.concatenate([msg_ref[i * 4 + u, 0:SLOTS, :] for u in range(4)], axis=0)
        num_t[...] += dot(values, weight[...], 0, 0)
        return carry

    lax.fori_loop(0, CTX // 4, merge, 0)

    xmsg[x, 0:WIDTH, :] = num_t[...].astype(BF16)
    den_high = den.astype(BF16).astype(F32)
    xmsg[x, WIDTH : WIDTH + 16, :] = jnp.concatenate(
        [top, den_high, den - den_high, jnp.zeros((13, ROWS), F32)], axis=0
    ).astype(BF16)
    pl.semaphore_wait(barrier, 1 + NX - 1 + NY - 1 + NZ - 1)
    copies = []
    for j in range(1, NX):
        cp = remote(xmsg.at[x], xmsg.at[x], x_send.at[j - 1], x_recv.at[j - 1], c, (x + j) % NX)
        cp.start()
        copies.append(cp)
    for cp in copies:
        cp.wait()
    tails = [xmsg[i, WIDTH : WIDTH + 16, :].astype(F32) for i in range(NX)]
    best = functools.reduce(jnp.maximum, [v[0:1] for v in tails])
    num, den = 0.0, 0.0
    for i in range(NX):
        f = jnp.exp2(tails[i][0:1] - best)
        den = den + f * (tails[i][1:2] + tails[i][2:3])
        num = num + f * xmsg[i, 0:WIDTH, :].astype(F32)
    att_t[...] = (num / den).astype(BF16)

    def half(v_ref, which):
        return v_ref[:, pl.ds(pl.multiple_of(which * 128, 128), 128)]

    def reduce_scatter(n, piece):
        core_out[n] = piece(1 - k).astype(BF16)
        cp = remote(core_out.at[n], core_in.at[n], c_send.at[n], c_recv.at[n], other, x)
        cp.start()
        mine = piece(k)
        cp.wait_recv()
        total = mine + core_in[n].astype(F32)
        y_out[n] = total.reshape(NY, 32, LOCAL).astype(BF16)
        pending = [cp]
        arrivals = []
        for j in range(1, NY):
            to = (y + j) % NY
            cp = remote(y_out.at[n, to], y_in.at[n, j - 1], y_send.at[n, j - 1], y_recv.at[n, j - 1], ctx_of(to, z, k), x)
            cp.start()
            pending.append(cp)
            arrivals.append(cp)
        acc = y_out[n, y].astype(F32)
        for j, cp in enumerate(arrivals):
            cp.wait_recv()
            acc = acc + y_in[n, j].astype(F32)
        regroup(acc, z_out.at[n])
        arrivals = []
        for j in range(1, NZ):
            to = (z + j) % NZ
            cp = remote(z_out.at[n, to], z_in.at[n, j - 1], z_send.at[n, j - 1], z_recv.at[n, j - 1], ctx_of(y, to, k), x)
            cp.start()
            pending.append(cp)
            arrivals.append(cp)
        acc = z_out[n, z].astype(F32)
        for j, cp in enumerate(arrivals):
            cp.wait_recv()
            acc = acc + z_in[n, j].astype(F32)
        return acc, pending

    loads[0].wait()
    projected, pending = reduce_scatter(0, lambda which: dot(half(att_t, which), wo[...], 0, 0))
    stream = (residual_ref[...].astype(F32) + projected).astype(BF16)
    stream_ref[...] = stream

    z_all[z] = stream
    arrivals = []
    for j in range(1, NZ):
        cp = remote(z_all.at[z], z_all.at[z], gz_send.at[j - 1], gz_recv.at[j - 1], ctx_of(y, (z + j) % NZ, k), x)
        cp.start()
        pending.append(cp)
        arrivals.append(cp)
    for cp in arrivals:
        cp.wait_recv()

    def put(b, v):
        x_all[k, y, :, b * 512 : (b + 1) * 512] = v

    ungroup(z_all, put)
    arrivals = []
    for j in range(1, NY):
        cp = remote(x_all.at[k, y], x_all.at[k, y], gy_send.at[j - 1], gy_recv.at[j - 1], ctx_of((y + j) % NY, z, k), x)
        cp.start()
        pending.append(cp)
        arrivals.append(cp)
    for cp in arrivals:
        cp.wait_recv()
    core_copy = remote(x_all.at[k], x_all.at[k], gc_send, gc_recv, other, x)
    core_copy.start()
    pending.append(core_copy)
    loads[1].wait()
    loads[2].wait()

    def gate_up(which):
        rows = x_all[which].reshape(128, LOCAL)
        wide = rows.astype(F32)
        squares = jnp.sum(wide * wide, axis=1, keepdims=True)
        scaled = (wide * gain_ref[...]).astype(BF16)
        for n, weight_ref in enumerate((wg, wu)):
            gu32[n, which, :, 0:UNITS] = dot(scaled, weight_ref[...], 1, 0).astype(BF16)
        high = squares.astype(BF16).astype(F32)
        lane = lax.broadcasted_iota(jnp.int32, (128, 256 - UNITS), 1)
        gu32[0, which, :, UNITS:256] = jnp.where(lane == 0, high, squares - high).astype(BF16)
        gu32[1, which, :, UNITS:256] = jnp.zeros((128, 256 - UNITS), BF16)

    gate_up(k)
    core_copy.wait_recv()
    gate_up(1 - k)

    for q in range(NX):
        for n in range(2):
            gu_out[q, n] = gu32[n, q // 2, (q % 2) * 64 : (q % 2) * 64 + 64, :]
    arrivals = []
    for j in range(1, NX):
        to = (x + j) % NX
        cp = remote(gu_out.at[to], gu_in.at[j - 1], r_send.at[j - 1], r_recv.at[j - 1], c, to)
        cp.start()
        pending.append(cp)
        arrivals.append(cp)
    acc = gu_out[x].astype(F32)
    for j, cp in enumerate(arrivals):
        cp.wait_recv()
        acc = acc + gu_in[j].astype(F32)
    squares = acc[0, :, UNITS : UNITS + 1] + acc[0, :, UNITS + 1 : UNITS + 2]
    factor = lax.rsqrt(squares / MODEL + EPS)
    gate = acc[0] * factor
    up = acc[1] * factor
    lane = lax.broadcasted_iota(jnp.int32, (64, 256), 1)
    hidden = jnp.where(lane < UNITS, gate / (1.0 + jnp.exp(-gate)) * up, 0.0)
    hid[x] = hidden.astype(BF16)
    arrivals = []
    for j in range(1, NX):
        cp = remote(hid.at[x], hid.at[x], h_send.at[j - 1], h_recv.at[j - 1], c, (x + j) % NX)
        cp.start()
        pending.append(cp)
        arrivals.append(cp)
    for cp in arrivals:
        cp.wait_recv()
    loads[3].wait()

    def down(which):
        rows = hid[pl.ds(which * 2, 2)].reshape(128, 256)
        return dot(rows, wd[...], 1, 0)

    updated, rest = reduce_scatter(1, down)
    update_ref[...] = updated.astype(BF16)
    for cp in pending + rest:
        cp.wait_send()


def prelude(chosen, p, head, mp):
    rows = jnp.arange(ROWS, dtype=jnp.int32)
    k, y, z, m = rows // 128, (rows // 32) % 4, (rows // 4) % 8, rows % 4
    pos_a = ((k * NX + m) * NY + y) * NZ + z
    pos_b = ((k * NY + y) * NX + m) * NZ + z
    ordered = chosen.reshape(HEADS, NY, NZ, NK, 4, 16).transpose(0, 3, 1, 2, 4, 5).reshape(HEADS, ROWS, 16)
    before = (rows[:, None] < rows[None, :]).astype(BF16)

    def ranks(member):
        count = jnp.dot(member.astype(BF16), before, preferred_element_type=F32)
        return jnp.where(member, count, -1.0)

    own = ranks(jnp.any(ordered == p, axis=2))
    spots = jnp.arange(SLOTS, dtype=F32)
    pos = jnp.where(jnp.arange(HEADS)[:, None] < 4, pos_a[None], pos_b[None])
    slots = jnp.sum(jnp.where(own[:, None, :] == spots[None, :, None], pos[:, None, :], 0), axis=2)
    listed = lax.dynamic_index_in_dim(ordered, head, 0, keepdims=False)
    ids = jnp.arange(CTX, dtype=jnp.int32) * NX + mp
    plane = ranks(jnp.any(listed[None] == ids[:, None, None], axis=2))
    return slots.reshape(-1).astype(jnp.int32), own, plane


def dma(*shape):
    return pltpu.SemaphoreType.DMA(shape)


def per_device(query, keys, values, chosen, residual, output_weight, norm_gain, gate_weight, up_weight, down_weight):
    c = lax.axis_index("ctx")
    x = lax.axis_index("mp")
    slots, own, plane = prelude(chosen, c * NX + x, c // GROUP, x)
    vmem = pl.BlockSpec(memory_space=pltpu.VMEM)
    hbm = pl.BlockSpec(memory_space=pl.ANY)
    messages = pl.pallas_call(
        attend_kernel,
        out_shape=jax.ShapeDtypeStruct((CTX, MSG, WIDTH), BF16),
        in_specs=[pl.BlockSpec(memory_space=pltpu.SMEM), vmem, vmem, hbm, hbm],
        out_specs=vmem,
        scratch_shapes=[
            pltpu.VMEM((4, ROWS, 16, WIDTH), BF16),
            pltpu.VMEM((HEADS, KEYS, WIDTH), BF16),
            pltpu.VMEM((HEADS, KEYS, WIDTH), BF16),
            pltpu.VMEM((SLOTS * GROUP, WIDTH), F32),
            pltpu.VMEM((SLOTS * GROUP, WIDTH), F32),
            pltpu.VMEM((SLOTS * GROUP, WIDTH), F32),
            pltpu.VMEM((CTX, MSG, WIDTH), BF16),
            dma(HEADS), dma(HEADS),
            dma(2, 7), dma(2, 7), dma(2, 3), dma(2, 3), dma(4, 3), dma(4, 3), dma(4, 4), dma(4, 4),
            dma(CTX), dma(CTX),
        ],
        compiler_params=pltpu.CompilerParams(collective_id=0, has_side_effects=True, vmem_limit_bytes=VMEM_LIMIT),
        name="attend",
    )(slots, query.reshape(4, 16, WIDTH), own, keys[0], values[0])
    fold = lambda a: a.reshape(4, 4, 512).transpose(1, 0, 2).reshape(16, 512)
    stream, update = pl.pallas_call(
        layer_kernel,
        out_shape=[jax.ShapeDtypeStruct((16, 512), BF16)] * 2,
        in_specs=[vmem, vmem, vmem, vmem, hbm, hbm, hbm, hbm],
        out_specs=[vmem, vmem],
        scratch_shapes=[
            pltpu.VMEM((WIDTH, LOCAL), BF16),
            pltpu.VMEM((LOCAL, UNITS), BF16),
            pltpu.VMEM((LOCAL, UNITS), BF16),
            pltpu.VMEM((256, LOCAL), BF16),
            pltpu.VMEM((4 * SLOTS, ROWS), BF16),
            pltpu.VMEM((CTX * 16, WIDTH), F32),
            pltpu.VMEM((CTX, ROWS), F32),
            pltpu.VMEM((WIDTH, ROWS), F32),
            pltpu.VMEM((NX, WIDTH + 16, ROWS), BF16),
            pltpu.VMEM((WIDTH, ROWS), BF16),
            pltpu.VMEM((2, 128, LOCAL), BF16),
            pltpu.VMEM((2, 128, LOCAL), BF16),
            pltpu.VMEM((2, NY, 32, LOCAL), BF16),
            pltpu.VMEM((2, NY - 1, 32, LOCAL), BF16),
            pltpu.VMEM((2, NZ, 16, 512), BF16),
            pltpu.VMEM((2, NZ - 1, 16, 512), BF16),
            pltpu.VMEM((NZ, 16, 512), BF16),
            pltpu.VMEM((NK, NY, 32, LOCAL), BF16),
            pltpu.VMEM((2, NK, 128, 256), BF16),
            pltpu.VMEM((NX, 2, 64, 256), BF16),
            pltpu.VMEM((NX - 1, 2, 64, 256), BF16),
            pltpu.VMEM((NX, 64, 256), BF16),
            dma(4), dma(3), dma(3),
            dma(2), dma(2), dma(2, 3), dma(2, 3), dma(2, 7), dma(2, 7),
            dma(7), dma(7), dma(3), dma(3), pltpu.SemaphoreType.DMA, pltpu.SemaphoreType.DMA,
            dma(3), dma(3), dma(3), dma(3),
        ],
        compiler_params=pltpu.CompilerParams(collective_id=1, has_side_effects=True, vmem_limit_bytes=VMEM_LIMIT),
        name="layer",
    )(messages, plane, fold(residual), norm_gain.reshape(1, LOCAL), output_weight, gate_weight, up_weight, down_weight)
    unfold = lambda a: a.reshape(4, 4, 512).transpose(1, 0, 2).reshape(4, LOCAL)
    return unfold(stream), unfold(update)


def solution(mesh):
    return jax.shard_map(
        per_device,
        mesh=mesh,
        in_specs=(
            P(("ctx", "mp"), None, None, None),
            P(("ctx", "mp"), None, None, None),
            P(("ctx", "mp"), None, None, None),
            P(),
            P("ctx", "mp"),
            P("ctx", "mp"),
            P("mp"),
            P("mp", "ctx"),
            P("mp", "ctx"),
            P("ctx", "mp"),
        ),
        out_specs=(P("ctx", "mp"), P("ctx", "mp")),
        check_vma=False,
    )
```

```python
import functools
import math

import jax
import jax.numpy as jnp
from jax import lax
from jax.experimental import pallas as pl
from jax.experimental.pallas import tpu as pltpu
from jax.sharding import PartitionSpec as P

NX, NY, NZ, NK = 4, 4, 8, 2
CTX = NY * NZ * NK
ROWS, HEADS, GROUP, WIDTH = 256, 8, 8, 128
KEYS, SLOTS = 2048, 64
MODEL, LOCAL, UNITS = 8192, 2048, 224
MSG = SLOTS + 16
EPS = 1e-5
LOWEST = -1e30
SCALE = WIDTH**-0.5 * math.log2(math.e)
MESH = pl.DeviceIdType.MESH
VMEM_LIMIT = 56 * 1024 * 1024
F32, BF16 = jnp.float32, jnp.bfloat16


def place():
    c = lax.axis_index("ctx")
    x = lax.axis_index("mp")
    return c, x, c // (NZ * NK), (c // NK) % NZ, c % NK


def ctx_of(y, z, k):
    return (y * NZ + z) * NK + k


def remote(src, dst, send_sem, recv_sem, ctx, mp):
    return pltpu.make_async_remote_copy(
        src_ref=src,
        dst_ref=dst,
        send_sem=send_sem,
        recv_sem=recv_sem,
        device_id=(ctx, mp),
        device_id_type=MESH,
    )


def dot(a, b, da, db):
    return lax.dot_general(a, b, (((da,), (db,)), ((), ())), preferred_element_type=F32)


def hp_at(t, y):
    return ((y // 2 + t % 2) % 2) * 2 + (y % 2 + t // 2) % 2


def layer_kernel(
    own_ref, chosen_ref, residual_ref, gain_ref, keys_ref, values_ref, wo_hbm, wg_hbm, wu_hbm, wd_hbm,
    stream_ref, update_ref,
    qbuf, qpair, kbuf, vbuf, q32, o32, st32, sendbuf, msg, picked, ranks, plane, slots_vmem, slots,
    wo, wg, wu, wd, weight, stats, running, num_t, xmsg, att_t,
    core_out, core_in, y_out, y_in, z_out, z_in,
    z_all, x_all, gu32, gu_out, gu_in, hid,
    k_sem, v_sem, s_sem,
    qz_send, qz_recv, p2_send, p2_recv, p3_send, p3_recv, qc_send, qc_recv,
    a_send, a_recv,
    w_sem, x_send, x_recv,
    c_send, c_recv, y_send, y_recv, z_send, z_recv,
    gz_send, gz_recv, gy_send, gy_recv, gc_send, gc_recv,
    r_send, r_recv, h_send, h_recv,
):
    c, x, y, z, k = place()
    other = ctx_of(y, z, 1 - k)
    pending = []

    barrier = pltpu.get_barrier_semaphore()
    pl.semaphore_signal(barrier, inc=1, device_id=(other, x), device_id_type=MESH)
    for j in range(1, NX):
        pl.semaphore_signal(barrier, inc=1, device_id=(c, (x + j) % NX), device_id_type=MESH)
    for j in range(1, NY):
        pl.semaphore_signal(barrier, inc=1, device_id=(ctx_of((y + j) % NY, z, k), x), device_id_type=MESH)
    for j in range(1, NZ):
        pl.semaphore_signal(barrier, inc=1, device_id=(ctx_of(y, (z + j) % NZ, k), x), device_id_type=MESH)

    def load(t, carry):
        h = hp_at(t // 2, y) * 2 + t % 2
        pltpu.make_async_copy(keys_ref.at[h], kbuf.at[h], k_sem.at[h]).start()
        pltpu.make_async_copy(values_ref.at[h], vbuf.at[h], v_sem.at[h]).start()
        return carry

    row_a = ((k * NX + x) * NY + y) * NZ
    row_b = ((k * NY + y) * NX + x) * NZ
    qbuf[0:2, row_a + z] = own_ref[0:2]
    qbuf[2:4, row_b + z] = own_ref[2:4]
    pl.semaphore_wait(barrier, 1 + NX - 1 + NY - 1 + NZ - 1)

    arrivals = []
    for j in range(1, NZ):
        to = ctx_of(y, (z + j) % NZ, k)
        for half, row in ((0, row_a), (1, row_b)):
            ref = qbuf.at[pl.ds(2 * half, 2), row + z]
            cp = remote(ref, ref, qz_send.at[half, j - 1], qz_recv.at[half, j - 1], to, x)
            cp.start()
            arrivals.append(cp)
    pending += arrivals
    lax.fori_loop(0, HEADS, load, 0)

    r_in = lax.broadcasted_iota(jnp.int32, (ROWS, ROWS), 0)
    r_out = lax.broadcasted_iota(jnp.int32, (ROWS, ROWS), 1)
    moved = ((r_in // 64) * 32 + ((r_in // 8) % 8) * 4 + r_in % 4) + ((r_in // 4) % 2) * 128
    permute = jnp.where(moved == r_out, 1.0, 0.0).astype(BF16)
    before = jnp.where(r_in < r_out, 1.0, 0.0).astype(BF16)
    listed = chosen_ref[...].reshape(HEADS * 16, ROWS).astype(F32).astype(BF16)
    picked[...] = dot(listed, permute, 1, 0)
    own_id = (c * NX + x).astype(F32)
    found = [
        jnp.max(jnp.where(picked[h * 16 : h * 16 + 16, :] == own_id, 1.0, 0.0), axis=0, keepdims=True)
        for h in range(HEADS)
    ]
    member = jnp.concatenate(found, axis=0)
    ranks[...] = jnp.where(member > 0.5, dot(jnp.concatenate([member, member], axis=0).astype(BF16), before, 1, 0)[0:HEADS], -1.0)
    ids = (lax.broadcasted_iota(jnp.int32, (CTX, ROWS), 0) * NX + x).astype(F32)
    member = jnp.zeros((CTX, ROWS), F32)
    for i in range(16):
        row = picked[pl.ds((c // GROUP) * 16 + i, 1), :]
        member = jnp.maximum(member, jnp.where(row == ids, 1.0, 0.0))
    plane[...] = jnp.where(member > 0.5, dot(member.astype(BF16), before, 1, 0), -1.0)
    r8 = lax.broadcasted_iota(jnp.int32, (16, ROWS), 1)
    kk, yy, zz, mm = r8 // 128, (r8 // 32) % 4, (r8 // 4) % 8, r8 % 4
    pos_a = (((kk * NX + mm) * NY + yy) * NZ + zz).astype(F32).astype(BF16)
    pos_b = (((kk * NY + yy) * NX + mm) * NZ + zz).astype(F32).astype(BF16)
    spot = lax.broadcasted_iota(jnp.int32, (128, ROWS), 0).astype(F32)
    for h in range(HEADS):
        hit = jnp.where(spot == ranks[h : h + 1, :], 1.0, 0.0).astype(BF16)
        at = dot(pos_a if h < 4 else pos_b, hit, 1, 1)
        slots_vmem[h : h + 1, :] = at[0:1].astype(jnp.int32)
    to_scalar = pltpu.make_async_copy(slots_vmem, slots, s_sem)
    to_scalar.start()
    for cp in arrivals:
        cp.wait_recv()

    arrivals = []
    for j in range(1, 4):
        ref = qbuf.at[0:2, pl.ds(row_a, NZ)]
        cp = remote(ref, ref, p2_send.at[0, j - 1], p2_recv.at[0, j - 1], ctx_of((y + j) % NY, z, k), x)
        cp.start()
        arrivals.append(cp)
        ref = qbuf.at[2:4, pl.ds(row_b, NZ)]
        cp = remote(ref, ref, p2_send.at[1, j - 1], p2_recv.at[1, j - 1], c, (x + j) % NX)
        cp.start()
        arrivals.append(cp)
    pending += arrivals
    for cp in arrivals:
        cp.wait_recv()

    def block(hp, n):
        return qbuf.at[hp, pl.ds(n * 32, 32)]

    def pass_on(hp, n, j):
        return remote(block(hp, n), block(hp, n), qc_send.at[hp, j], qc_recv.at[hp, j], other, x)

    for i in range(2):
        for j in range(1, 4):
            hp = (y % 2 + i) % 2
            ref = block(hp, k * NX + x)
            remote(ref, ref, p3_send.at[hp, j - 1], p3_recv.at[hp, j - 1], c, (x + j) % NX).start()
            to = (y + j) % NY
            hp = 2 + (to % 2 + i) % 2
            ref = block(hp, k * NY + y)
            remote(ref, ref, p3_send.at[hp, j - 1], p3_recv.at[hp, j - 1], ctx_of(to, z, k), x).start()
    for hp in range(4):
        pass_on(hp, k * 4 + (x if hp < 2 else y), 0).start()

    def forward(hp):
        late = hp // 2
        for j in range(1, 4):
            n = k * 4 + (x * (1 - late) + y * late - j + 4) % 4
            ref = block(hp, n)
            remote(ref, ref, p3_send.at[hp, j - 1], p3_recv.at[hp, j - 1], other, x).wait_recv()
            pass_on(hp, n, j).start()

    forward(hp_at(0, y))
    forward(hp_at(1, y))
    to_scalar.wait()
    slot_iota = lax.broadcasted_iota(jnp.int32, (SLOTS, ROWS), 0).astype(F32)

    def head(h):
        hp = h // 2
        upper = (h % 2) == 1
        pltpu.make_async_copy(keys_ref.at[h], kbuf.at[h], k_sem.at[h]).wait()
        pltpu.make_async_copy(values_ref.at[h], vbuf.at[h], v_sem.at[h]).wait()

        def pick(i, carry):
            for u in range(8):
                s = i * 8 + u
                row = jnp.minimum(jnp.maximum(slots[h, s], 0), ROWS - 1)
                tile = qpair[row].astype(F32)
                q32[pl.ds(pl.multiple_of(s * 8, 8), 8), :] = jnp.where(upper, tile[8:16], tile[0:8])
            return carry

        lax.fori_loop(0, SLOTS // 8, pick, 0)

        for b in range(2):
            at = pl.ds(b * 256, 256)
            s = dot(q32[at, :].astype(BF16), kbuf[h], 1, 1)
            top = (jnp.max(s, axis=1, keepdims=True) * SCALE).astype(BF16).astype(F32)
            p = jnp.exp2(s * SCALE - top)
            total = jnp.sum(p, axis=1, keepdims=True)
            o32[at, :] = dot(p.astype(BF16), vbuf[h], 1, 0)
            lane = lax.broadcasted_iota(jnp.int32, (256, WIDTH), 1)
            st32[at, :] = jnp.where(lane == 0, top, total)

        hit = slot_iota == ranks[pl.ds(h, 1), :]
        for g in range(GROUP):
            n = h * GROUP + g
            sendbuf[n, 0:SLOTS, :] = o32[pl.ds(g, SLOTS, stride=GROUP), :].astype(BF16)
            st = st32[pl.ds(g, SLOTS, stride=GROUP), :]
            top = jnp.sum(jnp.where(hit, st[:, 0:1], 0.0), axis=0, keepdims=True)
            total = jnp.sum(jnp.where(hit, st[:, 1:2], 0.0), axis=0, keepdims=True)
            high = total.astype(BF16).astype(F32)
            low = total - high
            tile = jnp.concatenate(
                [
                    top[:, :128], top[:, 128:], high[:, :128], high[:, 128:],
                    low[:, :128], low[:, 128:], jnp.zeros((10, 128), F32),
                ],
                axis=0,
            )
            sendbuf[n, SLOTS:MSG, :] = tile.astype(BF16)

            @pl.when(n != c)
            def _():
                remote(sendbuf.at[n], msg.at[c], a_send.at[n], a_recv.at[c], n, x).start()

            @pl.when(n == c)
            def _():
                msg[c] = sendbuf[n]

    def pair(t, carry):
        hp = hp_at(t, y)
        for j in range(4):
            pass_on(hp, 0, j).wait_recv()
        qpair[...] = qbuf[hp]
        lax.fori_loop(0, 2, lambda i, v: (head(hp * 2 + i), v)[1], 0)

        @pl.when(t < 2)
        def _():
            forward(hp_at(t + 2, y))

        return carry

    lax.fori_loop(0, 4, pair, 0)

    loads = [
        pltpu.make_async_copy(wo_hbm, wo, w_sem.at[0]),
        pltpu.make_async_copy(wg_hbm, wg, w_sem.at[1]),
        pltpu.make_async_copy(wu_hbm, wu, w_sem.at[2]),
        pltpu.make_async_copy(wd_hbm, wd.at[pl.ds(0, UNITS)], w_sem.at[3]),
    ]
    for cp in loads:
        cp.start()
    wd[UNITS:256, :] = jnp.zeros((256 - UNITS, LOCAL), BF16)

    num_t[...] = jnp.zeros_like(num_t)
    running[0:1, :] = jnp.full((1, ROWS), LOWEST, F32)
    running[1:2, :] = jnp.zeros((1, ROWS), F32)

    def merge(t, carry):
        base = hp_at(t, y) * (NZ * NK)

        def arrive(i, v):
            s = base + i

            @pl.when(s != c)
            def _():
                remote(sendbuf.at[s], msg.at[s], a_send.at[s], a_recv.at[s], s, x).wait_recv()

            return v

        lax.fori_loop(0, NZ * NK, arrive, 0)
        for i in range(NZ * NK):
            stats[i * 16 : i * 16 + 16, :] = msg[base + i, SLOTS:MSG, :].astype(F32)

        def row_of(n):
            return jnp.concatenate([stats[pl.ds(2 * n + i, NZ * NK, stride=16), :] for i in range(2)], axis=1)

        rank = plane[pl.ds(pl.multiple_of(base, 16), 16), :]
        listed = rank >= 0.0
        top_each = jnp.where(listed, row_of(0), LOWEST)
        old = running[0:1, :]
        top = jnp.maximum(old, jnp.max(top_each, axis=0, keepdims=True))
        keep = jnp.exp2(old - top)
        w = jnp.where(listed, jnp.exp2(top_each - top), 0.0).astype(BF16).astype(F32)
        running[0:1, :] = top
        running[1:2, :] = running[1:2, :] * keep + jnp.sum(w * (row_of(1) + row_of(2)), axis=0, keepdims=True)
        total = num_t[...] * keep
        for i in range(NZ * NK // 4):
            for u in range(4):
                s = i * 4 + u
                weight[s * SLOTS : (s + 1) * SLOTS, :] = jnp.where(
                    slot_iota == rank[s : s + 1, :], w[s : s + 1, :], 0.0
                ).astype(BF16)
            values = jnp.concatenate([msg[base + i * 4 + u, 0:SLOTS, :] for u in range(4)], axis=0)
            total = total + dot(values, weight[i * 4 * SLOTS : (i + 1) * 4 * SLOTS, :], 0, 0)
        num_t[...] = total
        return carry

    lax.fori_loop(0, 4, merge, 0)

    top, den = running[0:1, :], running[1:2, :]

    xmsg[x, 0:WIDTH, :] = num_t[...].astype(BF16)
    den_high = den.astype(BF16).astype(F32)
    xmsg[x, WIDTH : WIDTH + 16, :] = jnp.concatenate(
        [top, den_high, den - den_high, jnp.zeros((13, ROWS), F32)], axis=0
    ).astype(BF16)
    arrivals = []
    for j in range(1, NX):
        cp = remote(xmsg.at[x], xmsg.at[x], x_send.at[j - 1], x_recv.at[j - 1], c, (x + j) % NX)
        cp.start()
        arrivals.append(cp)
    pending += arrivals
    for cp in arrivals:
        cp.wait_recv()
    tails = [xmsg[i, WIDTH : WIDTH + 16, :].astype(F32) for i in range(NX)]
    best = functools.reduce(jnp.maximum, [v[0:1] for v in tails])
    num, den = 0.0, 0.0
    for i in range(NX):
        f = jnp.exp2(tails[i][0:1] - best)
        den = den + f * (tails[i][1:2] + tails[i][2:3])
        num = num + f * xmsg[i, 0:WIDTH, :].astype(F32)
    att_t[...] = (num / den).astype(BF16)

    def half(v_ref, which):
        return v_ref[:, pl.ds(pl.multiple_of(which * 128, 128), 128)]

    def reduce_scatter(n, piece):
        core_out[n] = piece(1 - k).astype(BF16)
        cp = remote(core_out.at[n], core_in.at[n], c_send.at[n], c_recv.at[n], other, x)
        cp.start()
        mine = piece(k)
        cp.wait_recv()
        total = mine + core_in[n].astype(F32)
        y_out[n] = total.reshape(NY, 32, LOCAL).astype(BF16)
        pending.append(cp)
        arrivals = []
        for j in range(1, NY):
            to = (y + j) % NY
            cp = remote(y_out.at[n, to], y_in.at[n, j - 1], y_send.at[n, j - 1], y_recv.at[n, j - 1], ctx_of(to, z, k), x)
            cp.start()
            pending.append(cp)
            arrivals.append(cp)
        acc = y_out[n, y].astype(F32)
        for j, cp in enumerate(arrivals):
            cp.wait_recv()
            acc = acc + y_in[n, j].astype(F32)
        regroup(acc, z_out.at[n])
        arrivals = []
        for j in range(1, NZ):
            to = (z + j) % NZ
            cp = remote(z_out.at[n, to], z_in.at[n, j - 1], z_send.at[n, j - 1], z_recv.at[n, j - 1], ctx_of(y, to, k), x)
            cp.start()
            pending.append(cp)
            arrivals.append(cp)
        acc = z_out[n, z].astype(F32)
        for j, cp in enumerate(arrivals):
            cp.wait_recv()
            acc = acc + z_in[n, j].astype(F32)
        return acc

    loads[0].wait()
    projected = reduce_scatter(0, lambda which: dot(half(att_t, which), wo[...], 0, 0))
    stream = (fold(residual_ref[...].astype(F32)) + projected).astype(BF16)
    unfold(stream.astype(F32), stream_ref)

    z_all[z] = stream
    arrivals = []
    for j in range(1, NZ):
        cp = remote(z_all.at[z], z_all.at[z], gz_send.at[j - 1], gz_recv.at[j - 1], ctx_of(y, (z + j) % NZ, k), x)
        cp.start()
        pending.append(cp)
        arrivals.append(cp)
    for cp in arrivals:
        cp.wait_recv()

    def put(b, v):
        x_all[k, y, :, b * 512 : (b + 1) * 512] = v

    ungroup(z_all, put)
    arrivals = []
    for j in range(1, NY):
        cp = remote(x_all.at[k, y], x_all.at[k, y], gy_send.at[j - 1], gy_recv.at[j - 1], ctx_of((y + j) % NY, z, k), x)
        cp.start()
        pending.append(cp)
        arrivals.append(cp)
    for cp in arrivals:
        cp.wait_recv()
    core_copy = remote(x_all.at[k], x_all.at[k], gc_send, gc_recv, other, x)
    core_copy.start()
    pending.append(core_copy)
    loads[1].wait()
    loads[2].wait()

    def gate_up(which):
        rows = x_all[which].reshape(128, LOCAL)
        wide = rows.astype(F32)
        squares = jnp.sum(wide * wide, axis=1, keepdims=True)
        scaled = (wide * gain_ref[...]).astype(BF16)
        for n, weight_ref in enumerate((wg, wu)):
            gu32[n, which, :, 0:UNITS] = dot(scaled, weight_ref[...], 1, 1).astype(BF16)
        high = squares.astype(BF16).astype(F32)
        lane = lax.broadcasted_iota(jnp.int32, (128, 256 - UNITS), 1)
        gu32[0, which, :, UNITS:256] = jnp.where(lane == 0, high, squares - high).astype(BF16)
        gu32[1, which, :, UNITS:256] = jnp.zeros((128, 256 - UNITS), BF16)

    gate_up(k)
    core_copy.wait_recv()
    gate_up(1 - k)

    for q in range(NX):
        for n in range(2):
            gu_out[q, n] = gu32[n, q // 2, (q % 2) * 64 : (q % 2) * 64 + 64, :]
    arrivals = []
    for j in range(1, NX):
        to = (x + j) % NX
        cp = remote(gu_out.at[to], gu_in.at[j - 1], r_send.at[j - 1], r_recv.at[j - 1], c, to)
        cp.start()
        pending.append(cp)
        arrivals.append(cp)
    acc = gu_out[x].astype(F32)
    for j, cp in enumerate(arrivals):
        cp.wait_recv()
        acc = acc + gu_in[j].astype(F32)
    squares = acc[0, :, UNITS : UNITS + 1] + acc[0, :, UNITS + 1 : UNITS + 2]
    factor = lax.rsqrt(squares / MODEL + EPS)
    gate = acc[0] * factor
    up = acc[1] * factor
    lane = lax.broadcasted_iota(jnp.int32, (64, 256), 1)
    hidden = jnp.where(lane < UNITS, gate / (1.0 + jnp.exp(-gate)) * up, 0.0)
    hid[x] = hidden.astype(BF16)
    arrivals = []
    for j in range(1, NX):
        cp = remote(hid.at[x], hid.at[x], h_send.at[j - 1], h_recv.at[j - 1], c, (x + j) % NX)
        cp.start()
        pending.append(cp)
        arrivals.append(cp)
    for cp in arrivals:
        cp.wait_recv()
    loads[3].wait()

    def down(which):
        rows = hid[pl.ds(which * 2, 2)].reshape(128, 256)
        return dot(rows, wd[...], 1, 0)

    updated = reduce_scatter(1, down)
    unfold(updated, update_ref)
    for cp in pending:
        cp.wait_send()
    for hp in range(4):
        for j in range(3):
            remote(block(hp, 0), block(hp, 0), p3_send.at[hp, j], p3_recv.at[hp, j], other, x).wait_send()
        for j in range(4):
            pass_on(hp, 0, j).wait_send()

    def sent(n, carry):
        @pl.when(n != c)
        def _():
            remote(sendbuf.at[n], msg.at[n], a_send.at[n], a_recv.at[n], n, x).wait_send()

        return carry

    lax.fori_loop(0, CTX, sent, 0)

def swap4(v):
    return pltpu.roll(v, 4, 1)


def fold(v):
    return jnp.concatenate([v[:, b * 512 : (b + 1) * 512] for b in range(4)], axis=0)


def unfold(v, out_ref):
    for b in range(4):
        out_ref[:, b * 512 : (b + 1) * 512] = v[4 * b : 4 * b + 4].astype(BF16)


def regroup(acc, out_ref):
    parts = [acc[:, b * 512 : (b + 1) * 512].reshape(4, 8, 512) for b in range(4)]
    lower = lax.broadcasted_iota(jnp.int32, (4, 8, 512), 1) < 4
    even = [jnp.where(lower, parts[b], swap4(parts[b + 1])) for b in (0, 2)]
    odd = [jnp.where(lower, swap4(parts[b]), parts[b + 1]) for b in (0, 2)]
    for t in range(4):
        out_ref[2 * t] = jnp.concatenate([even[0][t], even[1][t]], axis=0).astype(BF16)
        out_ref[2 * t + 1] = jnp.concatenate([odd[0][t], odd[1][t]], axis=0).astype(BF16)


def ungroup(src_ref, store):
    a = src_ref[...].astype(F32)
    lower = lax.broadcasted_iota(jnp.int32, (8, 512), 0) < 4
    columns = [[], [], [], []]
    for t in range(4):
        for q in range(2):
            e = a[2 * t, 8 * q : 8 * q + 8]
            o = a[2 * t + 1, 8 * q : 8 * q + 8]
            columns[2 * q].append(jnp.where(lower, e, pltpu.roll(o, 4, 0)))
            columns[2 * q + 1].append(jnp.where(lower, pltpu.roll(e, 4, 0), o))
    for b in range(4):
        store(b, jnp.concatenate(columns[b], axis=0).astype(BF16))


def dma(*shape):
    return pltpu.SemaphoreType.DMA(shape)


def per_device(query, keys, values, chosen, residual, output_weight, norm_gain, gate_weight, up_weight, down_weight):
    vmem = pl.BlockSpec(memory_space=pltpu.VMEM)
    hbm = pl.BlockSpec(memory_space=pl.ANY)
    half = 16 * 16
    return pl.pallas_call(
        layer_kernel,
        out_shape=[jax.ShapeDtypeStruct((4, LOCAL), BF16)] * 2,
        in_specs=[vmem, vmem, vmem, vmem, hbm, hbm, hbm, hbm, hbm, hbm],
        out_specs=[vmem, vmem],
        scratch_shapes=[
            pltpu.VMEM((4, ROWS, 16, WIDTH), BF16),
            pltpu.VMEM((ROWS, 16, WIDTH), BF16),
            pltpu.VMEM((HEADS, KEYS, WIDTH), BF16),
            pltpu.VMEM((HEADS, KEYS, WIDTH), BF16),
            pltpu.VMEM((SLOTS * GROUP, WIDTH), F32),
            pltpu.VMEM((SLOTS * GROUP, WIDTH), F32),
            pltpu.VMEM((SLOTS * GROUP, WIDTH), F32),
            pltpu.VMEM((CTX, MSG, WIDTH), BF16),
            pltpu.VMEM((CTX, MSG, WIDTH), BF16),
            pltpu.VMEM((HEADS * 16, ROWS), F32),
            pltpu.VMEM((HEADS, ROWS), F32),
            pltpu.VMEM((CTX, ROWS), F32),
            pltpu.VMEM((HEADS, 128), jnp.int32),
            pltpu.SMEM((HEADS, 128), jnp.int32),
            pltpu.VMEM((WIDTH, LOCAL), BF16),
            pltpu.VMEM((UNITS, LOCAL), BF16),
            pltpu.VMEM((UNITS, LOCAL), BF16),
            pltpu.VMEM((256, LOCAL), BF16),
            pltpu.VMEM((16 * SLOTS, ROWS), BF16),
            pltpu.VMEM((half, WIDTH), F32),
            pltpu.VMEM((8, ROWS), F32),
            pltpu.VMEM((WIDTH, ROWS), F32),
            pltpu.VMEM((NX, WIDTH + 16, ROWS), BF16),
            pltpu.VMEM((WIDTH, ROWS), BF16),
            pltpu.VMEM((2, 128, LOCAL), BF16),
            pltpu.VMEM((2, 128, LOCAL), BF16),
            pltpu.VMEM((2, NY, 32, LOCAL), BF16),
            pltpu.VMEM((2, NY - 1, 32, LOCAL), BF16),
            pltpu.VMEM((2, NZ, 16, 512), BF16),
            pltpu.VMEM((2, NZ - 1, 16, 512), BF16),
            pltpu.VMEM((NZ, 16, 512), BF16),
            pltpu.VMEM((NK, NY, 32, LOCAL), BF16),
            pltpu.VMEM((2, NK, 128, 256), BF16),
            pltpu.VMEM((NX, 2, 64, 256), BF16),
            pltpu.VMEM((NX - 1, 2, 64, 256), BF16),
            pltpu.VMEM((NX, 64, 256), BF16),
            dma(HEADS), dma(HEADS), pltpu.SemaphoreType.DMA,
            dma(2, 7), dma(2, 7), dma(2, 3), dma(2, 3), dma(4, 3), dma(4, 3), dma(4, 4), dma(4, 4),
            dma(CTX), dma(CTX),
            dma(4), dma(3), dma(3),
            dma(2), dma(2), dma(2, 3), dma(2, 3), dma(2, 7), dma(2, 7),
            dma(7), dma(7), dma(3), dma(3), pltpu.SemaphoreType.DMA, pltpu.SemaphoreType.DMA,
            dma(3), dma(3), dma(3), dma(3),
        ],
        compiler_params=pltpu.CompilerParams(collective_id=0, has_side_effects=True, vmem_limit_bytes=VMEM_LIMIT),
        name="layer",
    )(
        query.reshape(4, 16, WIDTH), chosen.transpose(0, 2, 1), residual, norm_gain.reshape(1, LOCAL),
        keys[0], values[0], output_weight, gate_weight.T, up_weight.T, down_weight,
    )


def solution(mesh):
    return jax.shard_map(
        per_device,
        mesh=mesh,
        in_specs=(
            P(("ctx", "mp"), None, None, None),
            P(("ctx", "mp"), None, None, None),
            P(("ctx", "mp"), None, None, None),
            P(),
            P("ctx", "mp"),
            P("ctx", "mp"),
            P("mp"),
            P("mp", "ctx"),
            P("mp", "ctx"),
            P("ctx", "mp"),
        ),
        out_specs=(P("ctx", "mp"), P("ctx", "mp")),
        check_vma=False,
    )
```

```python
import functools
import math

import jax
import jax.numpy as jnp
from jax import lax
from jax.experimental import pallas as pl
from jax.experimental.pallas import tpu as pltpu
from jax.sharding import PartitionSpec as P

NX, NY, NZ, NK = 4, 4, 8, 2
CTX = NY * NZ * NK
ROWS, HEADS, GROUP, WIDTH = 256, 8, 8, 128
KEYS, SLOTS = 2048, 64
MODEL, LOCAL, HALF, UNITS = 8192, 2048, 1024, 224
MSG = SLOTS + 16
EPS = 1e-5
LOWEST = -1e30
SCALE = WIDTH**-0.5 * math.log2(math.e)
MESH = pl.DeviceIdType.MESH
VMEM_LIMIT = 56 * 1024 * 1024
F32, BF16 = jnp.float32, jnp.bfloat16


def place():
    c = lax.axis_index("ctx")
    x = lax.axis_index("mp")
    return c, x, c // (NZ * NK), (c // NK) % NZ, c % NK


def ctx_of(y, z, k):
    return (y * NZ + z) * NK + k


def remote(src, dst, send_sem, recv_sem, ctx, mp):
    return pltpu.make_async_remote_copy(
        src_ref=src,
        dst_ref=dst,
        send_sem=send_sem,
        recv_sem=recv_sem,
        device_id=(ctx, mp),
        device_id_type=MESH,
    )


def dot(a, b, da, db):
    return lax.dot_general(a, b, (((da,), (db,)), ((), ())), preferred_element_type=F32)


def hp_at(t, y):
    return ((y // 2 + t % 2) % 2) * 2 + (y % 2 + t // 2) % 2


def layer_kernel(
    own_ref, chosen_ref, residual_ref, gain_ref, keys_ref, values_ref, wo_hbm, wg_hbm, wu_hbm, wd_hbm,
    stream_ref, update_ref,
    qbuf, qpair, kbuf, vbuf, q32, o32, st32, sendbuf, msg, picked, ranks, plane, slots_vmem, slots,
    wo, wg, wu, wd, weight, stats, running, num_t, xmsg, att_t,
    core_out, core_in, y_out, y_in, z_out, z_in,
    z_all, x_all, gu32, gu_out, gu_in, hid,
    k_sem, v_sem, s_sem,
    qz_send, qz_recv, p2_send, p2_recv, p3_send, p3_recv, p4_send, p4_recv, qc_send, qc_recv,
    a_send, a_recv,
    w_sem, x_send, x_recv,
    c_send, c_recv, y_send, y_recv, z_send, z_recv,
    gz_send, gz_recv, gy_send, gy_recv, gc_send, gc_recv,
    r_send, r_recv, h_send, h_recv,
):
    c, x, y, z, k = place()
    other = ctx_of(y, z, 1 - k)
    pending = []

    barrier = pltpu.get_barrier_semaphore()
    pl.semaphore_signal(barrier, inc=1, device_id=(other, x), device_id_type=MESH)
    for j in range(1, NX):
        pl.semaphore_signal(barrier, inc=1, device_id=(c, (x + j) % NX), device_id_type=MESH)
    for j in range(1, NY):
        pl.semaphore_signal(barrier, inc=1, device_id=(ctx_of((y + j) % NY, z, k), x), device_id_type=MESH)
    for j in range(1, NZ):
        pl.semaphore_signal(barrier, inc=1, device_id=(ctx_of(y, (z + j) % NZ, k), x), device_id_type=MESH)

    def load(t, carry):
        h = hp_at(t // 2, y) * 2 + t % 2
        pltpu.make_async_copy(keys_ref.at[h], kbuf.at[h], k_sem.at[h]).start()
        pltpu.make_async_copy(values_ref.at[h], vbuf.at[h], v_sem.at[h]).start()
        return carry

    row_a = ((k * NX + x) * NY + y) * NZ
    row_b = ((k * NY + y) * NX + x) * NZ
    qbuf[0:2, row_a + z] = own_ref[0:2]
    qbuf[2:4, row_b + z] = own_ref[2:4]
    pl.semaphore_wait(barrier, 1 + NX - 1 + NY - 1 + NZ - 1)

    arrivals = []
    for j in range(1, NZ):
        to = ctx_of(y, (z + j) % NZ, k)
        for half, row in ((0, row_a), (1, row_b)):
            ref = qbuf.at[pl.ds(2 * half, 2), row + z]
            cp = remote(ref, ref, qz_send.at[half, j - 1], qz_recv.at[half, j - 1], to, x)
            cp.start()
            arrivals.append(cp)
    pending += arrivals
    lax.fori_loop(0, HEADS, load, 0)

    loads = [
        pltpu.make_async_copy(wo_hbm, wo, w_sem.at[0]),
        pltpu.make_async_copy(wg_hbm, wg, w_sem.at[1]),
        pltpu.make_async_copy(wu_hbm, wu, w_sem.at[2]),
        pltpu.make_async_copy(wd_hbm, wd.at[pl.ds(0, UNITS)], w_sem.at[3]),
    ]
    for cp in loads:
        cp.start()
    wd[UNITS:256, :] = jnp.zeros((256 - UNITS, LOCAL), BF16)

    r_in = lax.broadcasted_iota(jnp.int32, (ROWS, ROWS), 0)
    r_out = lax.broadcasted_iota(jnp.int32, (ROWS, ROWS), 1)
    moved = ((r_in // 64) * 32 + ((r_in // 8) % 8) * 4 + r_in % 4) + ((r_in // 4) % 2) * 128
    permute = jnp.where(moved == r_out, 1.0, 0.0).astype(BF16)
    before = jnp.where(r_in < r_out, 1.0, 0.0).astype(BF16)
    listed = chosen_ref[...].reshape(HEADS * 16, ROWS).astype(F32).astype(BF16)
    picked[...] = dot(listed, permute, 1, 0)
    own_id = (c * NX + x).astype(F32)
    found = [
        jnp.max(jnp.where(picked[h * 16 : h * 16 + 16, :] == own_id, 1.0, 0.0), axis=0, keepdims=True)
        for h in range(HEADS)
    ]
    member = jnp.concatenate(found, axis=0)
    ranks[...] = jnp.where(member > 0.5, dot(jnp.concatenate([member, member], axis=0).astype(BF16), before, 1, 0)[0:HEADS], -1.0)
    ids = (lax.broadcasted_iota(jnp.int32, (CTX, ROWS), 0) * NX + x).astype(F32)
    member = jnp.zeros((CTX, ROWS), F32)
    for i in range(16):
        row = picked[pl.ds((c // GROUP) * 16 + i, 1), :]
        member = jnp.maximum(member, jnp.where(row == ids, 1.0, 0.0))
    plane[...] = jnp.where(member > 0.5, dot(member.astype(BF16), before, 1, 0), -1.0)
    r8 = lax.broadcasted_iota(jnp.int32, (16, ROWS), 1)
    kk, yy, zz, mm = r8 // 128, (r8 // 32) % 4, (r8 // 4) % 8, r8 % 4
    pos_a = (((kk * NX + mm) * NY + yy) * NZ + zz).astype(F32).astype(BF16)
    pos_b = (((kk * NY + yy) * NX + mm) * NZ + zz).astype(F32).astype(BF16)
    spot = lax.broadcasted_iota(jnp.int32, (128, ROWS), 0).astype(F32)
    for h in range(HEADS):
        hit = jnp.where(spot == ranks[h : h + 1, :], 1.0, 0.0).astype(BF16)
        at = dot(pos_a if h < 4 else pos_b, hit, 1, 1)
        slots_vmem[h : h + 1, :] = at[0:1].astype(jnp.int32)
    to_scalar = pltpu.make_async_copy(slots_vmem, slots, s_sem)
    to_scalar.start()
    for cp in arrivals:
        cp.wait_recv()

    arrivals = []
    for j in range(1, 4):
        ref = qbuf.at[0:2, pl.ds(row_a, NZ)]
        cp = remote(ref, ref, p2_send.at[0, j - 1], p2_recv.at[0, j - 1], ctx_of((y + j) % NY, z, k), x)
        cp.start()
        arrivals.append(cp)
        ref = qbuf.at[2:4, pl.ds(row_b, NZ)]
        cp = remote(ref, ref, p2_send.at[1, j - 1], p2_recv.at[1, j - 1], c, (x + j) % NX)
        cp.start()
        arrivals.append(cp)
    pending += arrivals

    def block(hp, n):
        return qbuf.at[hp, pl.ds(n * 32, 32)]

    def pass_on(hp, n, j):
        return remote(block(hp, n), block(hp, n), qc_send.at[hp, j], qc_recv.at[hp, j], other, x)

    def piece_of(hp, row, i, j):
        ref = qbuf.at[hp, pl.ds(row, NZ)]
        return ref, p4_send.at[hp, j - 1, i], p4_recv.at[hp, j - 1, i]

    for i in range(4):
        if i:
            for cp in arrivals[2 * i - 2 : 2 * i]:
                cp.wait_recv()
        for j in range(1, 4):
            ref, send, recv = piece_of(y % 2, ((k * NX + x) * NY + (y - i + NY) % NY) * NZ, i, j)
            remote(ref, ref, send, recv, c, (x + j) % NX).start()
            to = (y + j) % NY
            ref, send, recv = piece_of(2 + to % 2, ((k * NY + y) * NX + (x - i + NX) % NX) * NZ, i, j)
            remote(ref, ref, send, recv, ctx_of(to, z, k), x).start()
    for j in range(1, 4):
        hp = (y % 2 + 1) % 2
        ref = block(hp, k * NX + x)
        remote(ref, ref, p3_send.at[hp, j - 1], p3_recv.at[hp, j - 1], c, (x + j) % NX).start()
        to = (y + j) % NY
        hp = 2 + (to % 2 + 1) % 2
        ref = block(hp, k * NY + y)
        remote(ref, ref, p3_send.at[hp, j - 1], p3_recv.at[hp, j - 1], ctx_of(to, z, k), x).start()
    for hp in range(4):
        pass_on(hp, k * 4 + (x if hp < 2 else y), 0).start()

    def forward(hp, pieces):
        late = hp // 2
        for j in range(1, 4):
            n = k * 4 + (x * (1 - late) + y * late - j + 4) % 4
            ref = block(hp, n)
            if pieces:
                for i in range(4):
                    src, send, recv = piece_of(hp, n * 32, i, j)
                    remote(src, src, send, recv, other, x).wait_recv()
            else:
                remote(ref, ref, p3_send.at[hp, j - 1], p3_recv.at[hp, j - 1], other, x).wait_recv()
            pass_on(hp, n, j).start()

    forward(hp_at(0, y), True)
    forward(hp_at(1, y), True)
    to_scalar.wait()
    slot_iota = lax.broadcasted_iota(jnp.int32, (SLOTS, ROWS), 0).astype(F32)

    def head(h):
        hp = h // 2
        upper = (h % 2) == 1
        pltpu.make_async_copy(keys_ref.at[h], kbuf.at[h], k_sem.at[h]).wait()
        pltpu.make_async_copy(values_ref.at[h], vbuf.at[h], v_sem.at[h]).wait()

        def pick(i, carry):
            for u in range(8):
                s = i * 8 + u
                row = jnp.minimum(jnp.maximum(slots[h, s], 0), ROWS - 1)
                tile = qpair[row].astype(F32)
                q32[pl.ds(pl.multiple_of(s * 8, 8), 8), :] = jnp.where(upper, tile[8:16], tile[0:8])
            return carry

        lax.fori_loop(0, SLOTS // 8, pick, 0)

        for b in range(2):
            at = pl.ds(b * 256, 256)
            s = dot(q32[at, :].astype(BF16), kbuf[h], 1, 1)
            top = (jnp.max(s, axis=1, keepdims=True) * SCALE).astype(BF16).astype(F32)
            p = jnp.exp2(s * SCALE - top)
            total = jnp.sum(p, axis=1, keepdims=True)
            o32[at, :] = dot(p.astype(BF16), vbuf[h], 1, 0)
            lane = lax.broadcasted_iota(jnp.int32, (256, WIDTH), 1)
            st32[at, :] = jnp.where(lane == 0, top, total)

        hit = slot_iota == ranks[pl.ds(h, 1), :]
        for g in range(GROUP):
            n = h * GROUP + g
            sendbuf[n, 0:SLOTS, :] = o32[pl.ds(g, SLOTS, stride=GROUP), :].astype(BF16)
            st = st32[pl.ds(g, SLOTS, stride=GROUP), :]
            top = jnp.sum(jnp.where(hit, st[:, 0:1], 0.0), axis=0, keepdims=True)
            total = jnp.sum(jnp.where(hit, st[:, 1:2], 0.0), axis=0, keepdims=True)
            high = total.astype(BF16).astype(F32)
            low = total - high
            tile = jnp.concatenate(
                [
                    top[:, :128], top[:, 128:], high[:, :128], high[:, 128:],
                    low[:, :128], low[:, 128:], jnp.zeros((10, 128), F32),
                ],
                axis=0,
            )
            sendbuf[n, SLOTS:MSG, :] = tile.astype(BF16)

            @pl.when(n != c)
            def _():
                remote(sendbuf.at[n], msg.at[c], a_send.at[n], a_recv.at[c], n, x).start()

            @pl.when(n == c)
            def _():
                msg[c] = sendbuf[n]

    def pair(t, carry):
        hp = hp_at(t, y)
        for j in range(4):
            pass_on(hp, 0, j).wait_recv()
        qpair[...] = qbuf[hp]
        lax.fori_loop(0, 2, lambda i, v: (head(hp * 2 + i), v)[1], 0)

        @pl.when(t < 2)
        def _():
            forward(hp_at(t + 2, y), False)

        return carry

    lax.fori_loop(0, 4, pair, 0)

    num_t[...] = jnp.zeros_like(num_t)
    running[0:1, :] = jnp.full((1, ROWS), LOWEST, F32)
    running[1:2, :] = jnp.zeros((1, ROWS), F32)

    def merge(t, carry):
        base = hp_at(t, y) * (NZ * NK)

        def arrive(i, v):
            s = base + i

            @pl.when(s != c)
            def _():
                remote(sendbuf.at[s], msg.at[s], a_send.at[s], a_recv.at[s], s, x).wait_recv()

            return v

        lax.fori_loop(0, NZ * NK, arrive, 0)
        for i in range(NZ * NK):
            stats[i * 16 : i * 16 + 16, :] = msg[base + i, SLOTS:MSG, :].astype(F32)

        def row_of(n):
            return jnp.concatenate([stats[pl.ds(2 * n + i, NZ * NK, stride=16), :] for i in range(2)], axis=1)

        rank = plane[pl.ds(pl.multiple_of(base, 16), 16), :]
        listed = rank >= 0.0
        top_each = jnp.where(listed, row_of(0), LOWEST)
        old = running[0:1, :]
        top = jnp.maximum(old, jnp.max(top_each, axis=0, keepdims=True))
        keep = jnp.exp2(old - top)
        w = jnp.where(listed, jnp.exp2(top_each - top), 0.0).astype(BF16).astype(F32)
        running[0:1, :] = top
        running[1:2, :] = running[1:2, :] * keep + jnp.sum(w * (row_of(1) + row_of(2)), axis=0, keepdims=True)
        total = num_t[...] * keep
        for i in range(NZ * NK // 4):
            for u in range(4):
                s = i * 4 + u
                weight[s * SLOTS : (s + 1) * SLOTS, :] = jnp.where(
                    slot_iota == rank[s : s + 1, :], w[s : s + 1, :], 0.0
                ).astype(BF16)
            values = jnp.concatenate([msg[base + i * 4 + u, 0:SLOTS, :] for u in range(4)], axis=0)
            total = total + dot(values, weight[i * 4 * SLOTS : (i + 1) * 4 * SLOTS, :], 0, 0)
        num_t[...] = total
        return carry

    lax.fori_loop(0, 4, merge, 0)

    top, den = running[0:1, :], running[1:2, :]

    xmsg[x, 0:WIDTH, :] = num_t[...].astype(BF16)
    den_high = den.astype(BF16).astype(F32)
    xmsg[x, WIDTH : WIDTH + 16, :] = jnp.concatenate(
        [top, den_high, den - den_high, jnp.zeros((13, ROWS), F32)], axis=0
    ).astype(BF16)
    arrivals = []
    for j in range(1, NX):
        cp = remote(xmsg.at[x], xmsg.at[x], x_send.at[j - 1], x_recv.at[j - 1], c, (x + j) % NX)
        cp.start()
        arrivals.append(cp)
    pending += arrivals
    for cp in arrivals:
        cp.wait_recv()
    tails = [xmsg[i, WIDTH : WIDTH + 16, :].astype(F32) for i in range(NX)]
    best = functools.reduce(jnp.maximum, [v[0:1] for v in tails])
    num, den = 0.0, 0.0
    for i in range(NX):
        f = jnp.exp2(tails[i][0:1] - best)
        den = den + f * (tails[i][1:2] + tails[i][2:3])
        num = num + f * xmsg[i, 0:WIDTH, :].astype(F32)
    att_t[...] = (num / den).astype(BF16)

    def half(v_ref, which):
        return v_ref[:, pl.ds(pl.multiple_of(which * 128, 128), 128)]

    def reduce_scatter(n, piece, use):
        cores, along_y, along_z = [], [], []
        for h in range(2):
            core_out[n, h] = piece(1 - k, h).astype(BF16)
            cp = remote(core_out.at[n, h], core_in.at[n, h], c_send.at[n, h], c_recv.at[n, h], other, x)
            cp.start()
            cores.append(cp)
        for h in range(2):
            mine = piece(k, h)
            cores[h].wait_recv()
            total = mine + core_in[n, h].astype(F32)
            y_out[n, h] = total.reshape(NY, 32, HALF).astype(BF16)
            copies = []
            for j in range(1, NY):
                to = (y + j) % NY
                cp = remote(
                    y_out.at[n, h, to], y_in.at[n, h, j - 1], y_send.at[n, h, j - 1], y_recv.at[n, h, j - 1], ctx_of(to, z, k), x
                )
                cp.start()
                copies.append(cp)
            along_y.append(copies)
        for h in range(2):
            acc = y_out[n, h, y].astype(F32)
            for j, cp in enumerate(along_y[h]):
                cp.wait_recv()
                acc = acc + y_in[n, h, j].astype(F32)
            regroup(acc, z_out.at[n, h])
            copies = []
            for j in range(1, NZ):
                to = (z + j) % NZ
                cp = remote(
                    z_out.at[n, h, to], z_in.at[n, h, j - 1], z_send.at[n, h, j - 1], z_recv.at[n, h, j - 1], ctx_of(y, to, k), x
                )
                cp.start()
                copies.append(cp)
            along_z.append(copies)
        for h in range(2):
            acc = z_out[n, h, z].astype(F32)
            for j, cp in enumerate(along_z[h]):
                cp.wait_recv()
                acc = acc + z_in[n, h, j].astype(F32)
            use(h, acc)
        for copies in [cores] + along_y + along_z:
            pending.extend(copies)

    rows_z, rows_y, rows_c = [], [], []

    def spread(h, projected):
        stream = (fold(residual_ref[:, h * HALF : (h + 1) * HALF].astype(F32)) + projected).astype(BF16)
        z_all[h, z] = stream
        for j in range(1, NZ):
            cp = remote(z_all.at[h, z], z_all.at[h, z], gz_send.at[h, j - 1], gz_recv.at[h, j - 1], ctx_of(y, (z + j) % NZ, k), x)
            cp.start()
            rows_z.append(cp)
        unfold(stream.astype(F32), stream_ref, h)

    loads[0].wait()
    reduce_scatter(0, lambda which, h: dot(half(att_t, which), wo[:, h * HALF : (h + 1) * HALF], 0, 0), spread)
    for h in range(2):
        for cp in rows_z[h * (NZ - 1) : (h + 1) * (NZ - 1)]:
            cp.wait_recv()

        def put(b, v):
            x_all[h, k, y, :, b * 256 : (b + 1) * 256] = v

        ungroup(z_all.at[h], put)
        for j in range(1, NY):
            ref = x_all.at[h, k, y]
            cp = remote(ref, ref, gy_send.at[h, j - 1], gy_recv.at[h, j - 1], ctx_of((y + j) % NY, z, k), x)
            cp.start()
            rows_y.append(cp)

    def gate_up(which, h):
        wide = x_all[h, which].reshape(128, HALF).astype(F32)
        squares = jnp.sum(wide * wide, axis=1, keepdims=True)
        cut = slice(h * HALF, (h + 1) * HALF)
        scaled = (wide * gain_ref[:, cut]).astype(BF16)
        lane = lax.broadcasted_iota(jnp.int32, (128, 256 - UNITS), 1)
        parts = [dot(scaled, weight_ref[:, cut], 1, 1) for weight_ref in (wg, wu)]
        if h == 0:
            for n in range(2):
                gu32[n, which, :, 0:UNITS] = parts[n]
            gu32[0, which, :, UNITS:256] = jnp.where(lane < 2, squares, 0.0)
            gu32[1, which, :, UNITS:256] = jnp.zeros((128, 256 - UNITS), F32)
        else:
            for n in range(2):
                gu32[n, which, :, 0:UNITS] += parts[n]
            squares = squares + gu32[0, which, :, UNITS : UNITS + 1]
            high = squares.astype(BF16).astype(F32)
            gu32[0, which, :, UNITS:256] = jnp.where(lane == 0, high, squares - high)

    loads[1].wait()
    loads[2].wait()
    for h in range(2):
        for cp in rows_y[h * (NY - 1) : (h + 1) * (NY - 1)]:
            cp.wait_recv()
        cp = remote(x_all.at[h, k], x_all.at[h, k], gc_send.at[h], gc_recv.at[h], other, x)
        cp.start()
        rows_c.append(cp)
        gate_up(k, h)
    for h in range(2):
        rows_c[h].wait_recv()
        gate_up(1 - k, h)
    pending += rows_z + rows_y + rows_c

    for q in range(NX):
        for n in range(2):
            gu_out[q, n] = gu32[n, q // 2, (q % 2) * 64 : (q % 2) * 64 + 64, :].astype(BF16)
    arrivals = []
    for j in range(1, NX):
        to = (x + j) % NX
        cp = remote(gu_out.at[to], gu_in.at[j - 1], r_send.at[j - 1], r_recv.at[j - 1], c, to)
        cp.start()
        pending.append(cp)
        arrivals.append(cp)
    acc = gu_out[x].astype(F32)
    for j, cp in enumerate(arrivals):
        cp.wait_recv()
        acc = acc + gu_in[j].astype(F32)
    squares = acc[0, :, UNITS : UNITS + 1] + acc[0, :, UNITS + 1 : UNITS + 2]
    factor = lax.rsqrt(squares / MODEL + EPS)
    gate = acc[0] * factor
    up = acc[1] * factor
    lane = lax.broadcasted_iota(jnp.int32, (64, 256), 1)
    hidden = jnp.where(lane < UNITS, gate / (1.0 + jnp.exp(-gate)) * up, 0.0)
    hid[x] = hidden.astype(BF16)
    arrivals = []
    for j in range(1, NX):
        cp = remote(hid.at[x], hid.at[x], h_send.at[j - 1], h_recv.at[j - 1], c, (x + j) % NX)
        cp.start()
        pending.append(cp)
        arrivals.append(cp)
    for cp in arrivals:
        cp.wait_recv()
    loads[3].wait()

    def down(which, h):
        rows = hid[pl.ds(which * 2, 2)].reshape(128, 256)
        return dot(rows, wd[:, h * HALF : (h + 1) * HALF], 1, 0)

    reduce_scatter(1, down, lambda h, total: unfold(total, update_ref, h))
    for cp in pending:
        cp.wait_send()
    for j in range(1, 4):
        to = (y + j) % NY
        for first in (y % 2, 2 + to % 2):
            for i in range(4):
                src, send, recv = piece_of(first, 0, i, j)
                remote(src, src, send, recv, other, x).wait_send()
        for hp in ((y % 2 + 1) % 2, 2 + (to % 2 + 1) % 2):
            remote(block(hp, 0), block(hp, 0), p3_send.at[hp, j - 1], p3_recv.at[hp, j - 1], other, x).wait_send()
    for hp in range(4):
        for j in range(4):
            pass_on(hp, 0, j).wait_send()

    def sent(n, carry):
        @pl.when(n != c)
        def _():
            remote(sendbuf.at[n], msg.at[n], a_send.at[n], a_recv.at[n], n, x).wait_send()

        return carry

    lax.fori_loop(0, CTX, sent, 0)

def swap4(v):
    return pltpu.roll(v, 4, 1)


def fold(v):
    return jnp.concatenate([v[:, b * 256 : (b + 1) * 256] for b in range(4)], axis=0)


def unfold(v, out_ref, h):
    for b in range(4):
        at = h * HALF + b * 256
        out_ref[:, at : at + 256] = v[4 * b : 4 * b + 4].astype(BF16)


def regroup(acc, out_ref):
    parts = [acc[:, b * 256 : (b + 1) * 256].reshape(4, 8, 256) for b in range(4)]
    lower = lax.broadcasted_iota(jnp.int32, (4, 8, 256), 1) < 4
    even = [jnp.where(lower, parts[b], swap4(parts[b + 1])) for b in (0, 2)]
    odd = [jnp.where(lower, swap4(parts[b]), parts[b + 1]) for b in (0, 2)]
    for t in range(4):
        out_ref[2 * t] = jnp.concatenate([even[0][t], even[1][t]], axis=0).astype(BF16)
        out_ref[2 * t + 1] = jnp.concatenate([odd[0][t], odd[1][t]], axis=0).astype(BF16)


def ungroup(src_ref, store):
    a = src_ref[...].astype(F32)
    lower = lax.broadcasted_iota(jnp.int32, (8, 256), 0) < 4
    columns = [[], [], [], []]
    for t in range(4):
        for q in range(2):
            e = a[2 * t, 8 * q : 8 * q + 8]
            o = a[2 * t + 1, 8 * q : 8 * q + 8]
            columns[2 * q].append(jnp.where(lower, e, pltpu.roll(o, 4, 0)))
            columns[2 * q + 1].append(jnp.where(lower, pltpu.roll(e, 4, 0), o))
    for b in range(4):
        store(b, jnp.concatenate(columns[b], axis=0).astype(BF16))


def hand_out(stream_in, update_in, stream_ref, update_ref):
    stream_ref[...] = stream_in[...]
    update_ref[...] = update_in[...]


def dma(*shape):
    return pltpu.SemaphoreType.DMA(shape)


def per_device(query, keys, values, chosen, residual, output_weight, norm_gain, gate_weight, up_weight, down_weight):
    vmem = pl.BlockSpec(memory_space=pltpu.VMEM)
    hbm = pl.BlockSpec(memory_space=pl.ANY)
    half = 16 * 16
    stream, update = pl.pallas_call(
        layer_kernel,
        out_shape=[jax.ShapeDtypeStruct((4, LOCAL), BF16)] * 2,
        in_specs=[vmem, vmem, vmem, vmem, hbm, hbm, hbm, hbm, hbm, hbm],
        out_specs=[vmem, vmem],
        scratch_shapes=[
            pltpu.VMEM((4, ROWS, 16, WIDTH), BF16),
            pltpu.VMEM((ROWS, 16, WIDTH), BF16),
            pltpu.VMEM((HEADS, KEYS, WIDTH), BF16),
            pltpu.VMEM((HEADS, KEYS, WIDTH), BF16),
            pltpu.VMEM((SLOTS * GROUP, WIDTH), F32),
            pltpu.VMEM((SLOTS * GROUP, WIDTH), F32),
            pltpu.VMEM((SLOTS * GROUP, WIDTH), F32),
            pltpu.VMEM((CTX, MSG, WIDTH), BF16),
            pltpu.VMEM((CTX, MSG, WIDTH), BF16),
            pltpu.VMEM((HEADS * 16, ROWS), F32),
            pltpu.VMEM((HEADS, ROWS), F32),
            pltpu.VMEM((CTX, ROWS), F32),
            pltpu.VMEM((HEADS, 128), jnp.int32),
            pltpu.SMEM((HEADS, 128), jnp.int32),
            pltpu.VMEM((WIDTH, LOCAL), BF16),
            pltpu.VMEM((UNITS, LOCAL), BF16),
            pltpu.VMEM((UNITS, LOCAL), BF16),
            pltpu.VMEM((256, LOCAL), BF16),
            pltpu.VMEM((16 * SLOTS, ROWS), BF16),
            pltpu.VMEM((half, WIDTH), F32),
            pltpu.VMEM((8, ROWS), F32),
            pltpu.VMEM((WIDTH, ROWS), F32),
            pltpu.VMEM((NX, WIDTH + 16, ROWS), BF16),
            pltpu.VMEM((WIDTH, ROWS), BF16),
            pltpu.VMEM((2, 2, 128, HALF), BF16),
            pltpu.VMEM((2, 2, 128, HALF), BF16),
            pltpu.VMEM((2, 2, NY, 32, HALF), BF16),
            pltpu.VMEM((2, 2, NY - 1, 32, HALF), BF16),
            pltpu.VMEM((2, 2, NZ, 16, 256), BF16),
            pltpu.VMEM((2, 2, NZ - 1, 16, 256), BF16),
            pltpu.VMEM((2, NZ, 16, 256), BF16),
            pltpu.VMEM((2, NK, NY, 32, HALF), BF16),
            pltpu.VMEM((2, NK, 128, 256), F32),
            pltpu.VMEM((NX, 2, 64, 256), BF16),
            pltpu.VMEM((NX - 1, 2, 64, 256), BF16),
            pltpu.VMEM((NX, 64, 256), BF16),
            dma(HEADS), dma(HEADS), pltpu.SemaphoreType.DMA,
            dma(2, 7), dma(2, 7), dma(2, 3), dma(2, 3), dma(4, 3), dma(4, 3), dma(4, 3, 4), dma(4, 3, 4), dma(4, 4), dma(4, 4),
            dma(CTX), dma(CTX),
            dma(4), dma(3), dma(3),
            dma(2, 2), dma(2, 2), dma(2, 2, 3), dma(2, 2, 3), dma(2, 2, 7), dma(2, 2, 7),
            dma(2, 7), dma(2, 7), dma(2, 3), dma(2, 3), dma(2), dma(2),
            dma(3), dma(3), dma(3), dma(3),
        ],
        compiler_params=pltpu.CompilerParams(collective_id=0, has_side_effects=True, vmem_limit_bytes=VMEM_LIMIT),
        name="layer",
    )(
        query.reshape(4, 16, WIDTH), chosen.transpose(0, 2, 1), residual, norm_gain.reshape(1, LOCAL),
        keys[0], values[0], output_weight, gate_weight.T, up_weight.T, down_weight,
    )
    return pl.pallas_call(
        hand_out,
        out_shape=[jax.ShapeDtypeStruct((4, LOCAL), BF16)] * 2,
        in_specs=[vmem, vmem],
        out_specs=[vmem, vmem],
        name="hand_out",
    )(stream, update)


def solution(mesh):
    return jax.shard_map(
        per_device,
        mesh=mesh,
        in_specs=(
            P(("ctx", "mp"), None, None, None),
            P(("ctx", "mp"), None, None, None),
            P(("ctx", "mp"), None, None, None),
            P(),
            P("ctx", "mp"),
            P("ctx", "mp"),
            P("mp"),
            P("mp", "ctx"),
            P("mp", "ctx"),
            P("ctx", "mp"),
        ),
        out_specs=(P("ctx", "mp"), P("ctx", "mp")),
        check_vma=False,
    )
```

```python
import functools
import math

import jax
import jax.numpy as jnp
from jax import lax
from jax.experimental import pallas as pl
from jax.experimental.pallas import tpu as pltpu
from jax.sharding import PartitionSpec as P

NX, NY, NZ, NK = 4, 4, 8, 2
CTX = NY * NZ * NK
ROWS, HEADS, GROUP, WIDTH = 256, 8, 8, 128
KEYS, SLOTS = 2048, 64
MODEL, LOCAL, HALF, UNITS = 8192, 2048, 1024, 224
EPS = 1e-5
LOWEST = -1e30
SCALE = WIDTH**-0.5 * math.log2(math.e)
MESH = pl.DeviceIdType.MESH
VMEM_LIMIT = 56 * 1024 * 1024
F32, BF16 = jnp.float32, jnp.bfloat16


def place():
    c = lax.axis_index("ctx")
    x = lax.axis_index("mp")
    return c, x, c // (NZ * NK), (c // NK) % NZ, c % NK


def ctx_of(y, z, k):
    return (y * NZ + z) * NK + k


def remote(src, dst, send_sem, recv_sem, ctx, mp):
    return pltpu.make_async_remote_copy(
        src_ref=src,
        dst_ref=dst,
        send_sem=send_sem,
        recv_sem=recv_sem,
        device_id=(ctx, mp),
        device_id_type=MESH,
    )


def dot(a, b, da, db):
    return lax.dot_general(a, b, (((da,), (db,)), ((), ())), preferred_element_type=F32)


def hp_at(t, y):
    return ((y // 2 + t % 2) % 2) * 2 + (y % 2 + t // 2) % 2


def layer_kernel(
    own_hbm, chosen_hbm, residual_ref, gain_hbm, keys_ref, values_ref, wo_hbm, wg_hbm, wu_hbm, wd_hbm,
    stream_ref, update_ref,
    own_ref, chosen_ref, gain_ref, qbuf, qpair, kbuf, vbuf, q32, o32, st32, sendbuf, msg, tops_out, tops_in, picked, ranks, plane, slots_vmem, slots,
    wo, wg, wu, wd, weight, stats, running, num_t, xmsg, att_t,
    core_out, core_in, y_out, y_in, z_out, z_in,
    z_all, x_all, gu32, gu_out, gu_in, hid,
    k_sem, v_sem, s_sem,
    qz_send, qz_recv, p2_send, p2_recv, p3_send, p3_recv, p4_send, p4_recv, qc_send, qc_recv,
    a_send, a_recv, b_send, b_recv, i_sem,
    w_sem, x_send, x_recv,
    c_send, c_recv, y_send, y_recv, z_send, z_recv,
    gz_send, gz_recv, gy_send, gy_recv, gc_send, gc_recv,
    r_send, r_recv, h_send, h_recv,
):
    c, x, y, z, k = place()
    other = ctx_of(y, z, 1 - k)
    pending = []

    barrier = pltpu.get_barrier_semaphore()
    pl.semaphore_signal(barrier, inc=1, device_id=(other, x), device_id_type=MESH)
    for j in range(1, NX):
        pl.semaphore_signal(barrier, inc=1, device_id=(c, (x + j) % NX), device_id_type=MESH)
    for j in range(1, NY):
        pl.semaphore_signal(barrier, inc=1, device_id=(ctx_of((y + j) % NY, z, k), x), device_id_type=MESH)
    for j in range(1, NZ):
        pl.semaphore_signal(barrier, inc=1, device_id=(ctx_of(y, (z + j) % NZ, k), x), device_id_type=MESH)

    def load(t, carry):
        h = hp_at(t // 2, y) * 2 + t % 2
        pltpu.make_async_copy(keys_ref.at[h], kbuf.at[h], k_sem.at[h]).start()
        pltpu.make_async_copy(values_ref.at[h], vbuf.at[h], v_sem.at[h]).start()
        return carry

    row_a = ((k * NX + x) * NY + y) * NZ
    row_b = ((k * NY + y) * NX + x) * NZ
    given = [
        pltpu.make_async_copy(own_hbm, own_ref, i_sem.at[0]),
        pltpu.make_async_copy(chosen_hbm, chosen_ref, i_sem.at[1]),
        pltpu.make_async_copy(gain_hbm, gain_ref, i_sem.at[2]),
    ]
    for cp in given:
        cp.start()
    given[0].wait()
    qbuf[0:2, row_a + z] = own_ref[0:2]
    qbuf[2:4, row_b + z] = own_ref[2:4]
    pl.semaphore_wait(barrier, 1 + NX - 1 + NY - 1 + NZ - 1)

    arrivals = []
    for j in range(1, NZ):
        to = ctx_of(y, (z + j) % NZ, k)
        for half, row in ((0, row_a), (1, row_b)):
            ref = qbuf.at[pl.ds(2 * half, 2), row + z]
            cp = remote(ref, ref, qz_send.at[half, j - 1], qz_recv.at[half, j - 1], to, x)
            cp.start()
            arrivals.append(cp)
    pending += arrivals
    lax.fori_loop(0, HEADS, load, 0)

    loads = [
        pltpu.make_async_copy(wo_hbm, wo, w_sem.at[0]),
        pltpu.make_async_copy(wg_hbm, wg, w_sem.at[1]),
        pltpu.make_async_copy(wu_hbm, wu, w_sem.at[2]),
        pltpu.make_async_copy(wd_hbm, wd.at[pl.ds(0, UNITS)], w_sem.at[3]),
    ]
    for cp in loads:
        cp.start()
    wd[UNITS:256, :] = jnp.zeros((256 - UNITS, LOCAL), BF16)

    for cp in given[1:]:
        cp.wait()

    r_in = lax.broadcasted_iota(jnp.int32, (ROWS, ROWS), 0)
    r_out = lax.broadcasted_iota(jnp.int32, (ROWS, ROWS), 1)
    moved = ((r_in // 64) * 32 + ((r_in // 8) % 8) * 4 + r_in % 4) + ((r_in // 4) % 2) * 128
    permute = jnp.where(moved == r_out, 1.0, 0.0).astype(BF16)
    before = jnp.where(r_in < r_out, 1.0, 0.0).astype(BF16)
    listed = chosen_ref[...].reshape(HEADS * 16, ROWS).astype(F32).astype(BF16)
    picked[...] = dot(listed, permute, 1, 0)
    own_id = (c * NX + x).astype(F32)
    found = [
        jnp.max(jnp.where(picked[h * 16 : h * 16 + 16, :] == own_id, 1.0, 0.0), axis=0, keepdims=True)
        for h in range(HEADS)
    ]
    member = jnp.concatenate(found, axis=0)
    ranks[...] = jnp.where(member > 0.5, dot(jnp.concatenate([member, member], axis=0).astype(BF16), before, 1, 0)[0:HEADS], -1.0)
    ids = (lax.broadcasted_iota(jnp.int32, (CTX, ROWS), 0) * NX + x).astype(F32)
    member = jnp.zeros((CTX, ROWS), F32)
    for i in range(16):
        row = picked[pl.ds((c // GROUP) * 16 + i, 1), :]
        member = jnp.maximum(member, jnp.where(row == ids, 1.0, 0.0))
    plane[...] = jnp.where(member > 0.5, dot(member.astype(BF16), before, 1, 0), -1.0)
    r8 = lax.broadcasted_iota(jnp.int32, (16, ROWS), 1)
    kk, yy, zz, mm = r8 // 128, (r8 // 32) % 4, (r8 // 4) % 8, r8 % 4
    pos_a = (((kk * NX + mm) * NY + yy) * NZ + zz).astype(F32).astype(BF16)
    pos_b = (((kk * NY + yy) * NX + mm) * NZ + zz).astype(F32).astype(BF16)
    spot = lax.broadcasted_iota(jnp.int32, (128, ROWS), 0).astype(F32)
    for h in range(HEADS):
        hit = jnp.where(spot == ranks[h : h + 1, :], 1.0, 0.0).astype(BF16)
        at = dot(pos_a if h < 4 else pos_b, hit, 1, 1)
        slots_vmem[h : h + 1, :] = at[0:1].astype(jnp.int32)
    to_scalar = pltpu.make_async_copy(slots_vmem, slots, s_sem)
    to_scalar.start()
    for cp in arrivals:
        cp.wait_recv()

    arrivals = []
    for j in range(1, 4):
        ref = qbuf.at[0:2, pl.ds(row_a, NZ)]
        cp = remote(ref, ref, p2_send.at[0, j - 1], p2_recv.at[0, j - 1], ctx_of((y + j) % NY, z, k), x)
        cp.start()
        arrivals.append(cp)
        ref = qbuf.at[2:4, pl.ds(row_b, NZ)]
        cp = remote(ref, ref, p2_send.at[1, j - 1], p2_recv.at[1, j - 1], c, (x + j) % NX)
        cp.start()
        arrivals.append(cp)
    pending += arrivals

    def block(hp, n):
        return qbuf.at[hp, pl.ds(n * 32, 32)]

    def pass_on(hp, n, j):
        return remote(block(hp, n), block(hp, n), qc_send.at[hp, j], qc_recv.at[hp, j], other, x)

    def piece_of(hp, row, i, j):
        ref = qbuf.at[hp, pl.ds(row, NZ)]
        return ref, p4_send.at[hp, j - 1, i], p4_recv.at[hp, j - 1, i]

    for i in range(4):
        if i:
            for cp in arrivals[2 * i - 2 : 2 * i]:
                cp.wait_recv()
        for j in range(1, 4):
            ref, send, recv = piece_of(y % 2, ((k * NX + x) * NY + (y - i + NY) % NY) * NZ, i, j)
            remote(ref, ref, send, recv, c, (x + j) % NX).start()
            to = (y + j) % NY
            ref, send, recv = piece_of(2 + to % 2, ((k * NY + y) * NX + (x - i + NX) % NX) * NZ, i, j)
            remote(ref, ref, send, recv, ctx_of(to, z, k), x).start()
    for j in range(1, 4):
        hp = (y % 2 + 1) % 2
        ref = block(hp, k * NX + x)
        remote(ref, ref, p3_send.at[hp, j - 1], p3_recv.at[hp, j - 1], c, (x + j) % NX).start()
        to = (y + j) % NY
        hp = 2 + (to % 2 + 1) % 2
        ref = block(hp, k * NY + y)
        remote(ref, ref, p3_send.at[hp, j - 1], p3_recv.at[hp, j - 1], ctx_of(to, z, k), x).start()
    for hp in range(4):
        pass_on(hp, k * 4 + (x if hp < 2 else y), 0).start()

    def forward(hp, pieces):
        late = hp // 2
        for j in range(1, 4):
            n = k * 4 + (x * (1 - late) + y * late - j + 4) % 4
            ref = block(hp, n)
            if pieces:
                for i in range(4):
                    src, send, recv = piece_of(hp, n * 32, i, j)
                    remote(src, src, send, recv, other, x).wait_recv()
            else:
                remote(ref, ref, p3_send.at[hp, j - 1], p3_recv.at[hp, j - 1], other, x).wait_recv()
            pass_on(hp, n, j).start()

    forward(hp_at(0, y), True)
    forward(hp_at(1, y), True)
    to_scalar.wait()
    slot_iota = lax.broadcasted_iota(jnp.int32, (SLOTS, ROWS), 0).astype(F32)

    def head(h):
        hp = h // 2
        upper = (h % 2) == 1
        pltpu.make_async_copy(keys_ref.at[h], kbuf.at[h], k_sem.at[h]).wait()
        pltpu.make_async_copy(values_ref.at[h], vbuf.at[h], v_sem.at[h]).wait()

        def pick(i, carry):
            for u in range(8):
                s = i * 8 + u
                row = jnp.minimum(jnp.maximum(slots[h, s], 0), ROWS - 1)
                tile = qpair[row].astype(F32)
                q32[pl.ds(pl.multiple_of(s * 8, 8), 8), :] = jnp.where(upper, tile[8:16], tile[0:8])
            return carry

        lax.fori_loop(0, SLOTS // 8, pick, 0)

        for b in range(2):
            at = pl.ds(b * 256, 256)
            s = dot(q32[at, :].astype(BF16), kbuf[h], 1, 1)
            top = (jnp.max(s, axis=1, keepdims=True) * SCALE).astype(BF16).astype(F32)
            p = jnp.exp2(s * SCALE - top)
            total = jnp.sum(p, axis=1, keepdims=True)
            o32[at, :] = dot(p.astype(BF16), vbuf[h], 1, 0)
            lane = lax.broadcasted_iota(jnp.int32, (256, WIDTH), 1)
            st32[at, :] = jnp.where(lane == 0, top, total)

        lane = lax.broadcasted_iota(jnp.int32, (SLOTS, WIDTH), 1)
        slot = lax.broadcasted_iota(jnp.int32, (SLOTS, WIDTH), 0)
        for g in range(GROUP):
            n = h * GROUP + g
            sendbuf[n] = o32[pl.ds(g, SLOTS, stride=GROUP), :].astype(BF16)
            st = st32[pl.ds(g, SLOTS, stride=GROUP), :]
            spread = jnp.where(lane == slot, st[:, 0:1], jnp.where(lane == slot + SLOTS, st[:, 1:2], 0.0))
            tops_out[n] = jnp.sum(spread, axis=0, keepdims=True)

            @pl.when(n != c)
            def _():
                remote(sendbuf.at[n], msg.at[c], a_send.at[n], a_recv.at[c], n, x).start()
                remote(tops_out.at[n], tops_in.at[c], b_send.at[n], b_recv.at[c], n, x).start()

            @pl.when(n == c)
            def _():
                msg[c] = sendbuf[n]
                tops_in[c] = tops_out[n]

    def pair(t, carry):
        hp = hp_at(t, y)
        for j in range(4):
            pass_on(hp, 0, j).wait_recv()
        qpair[...] = qbuf[hp]
        lax.fori_loop(0, 2, lambda i, v: (head(hp * 2 + i), v)[1], 0)

        @pl.when(t < 2)
        def _():
            forward(hp_at(t + 2, y), False)

        return carry

    lax.fori_loop(0, 4, pair, 0)

    num_t[...] = jnp.zeros_like(num_t)
    running[0:1, :] = jnp.full((1, ROWS), LOWEST, F32)
    running[1:2, :] = jnp.zeros((1, ROWS), F32)

    def merge(t, carry):
        base = hp_at(t, y) * (NZ * NK)

        def arrive(i, v):
            s = base + i

            @pl.when(s != c)
            def _():
                remote(sendbuf.at[s], msg.at[s], a_send.at[s], a_recv.at[s], s, x).wait_recv()
                remote(tops_out.at[s], tops_in.at[s], b_send.at[s], b_recv.at[s], s, x).wait_recv()

            return v

        lax.fori_loop(0, NZ * NK, arrive, 0)
        for i in range(NZ * NK):
            stats[i : i + 1, :] = tops_in[base + i]
        held = stats[...]
        rank = plane[pl.ds(pl.multiple_of(base, 16), 16), :]
        at = jnp.maximum(rank, 0.0).astype(jnp.int32)

        def by_row(first):
            return jnp.concatenate(
                [
                    jnp.take_along_axis(held, at[:, i * 128 : (i + 1) * 128] + first, axis=1, mode="promise_in_bounds")
                    for i in range(2)
                ],
                axis=1,
            )

        listed = rank >= 0.0
        top_each = jnp.where(listed, by_row(0), LOWEST)
        old = running[0:1, :]
        top = jnp.maximum(old, jnp.max(top_each, axis=0, keepdims=True))
        keep = jnp.exp2(old - top)
        w = jnp.where(listed, jnp.exp2(top_each - top), 0.0).astype(BF16).astype(F32)
        running[0:1, :] = top
        running[1:2, :] = running[1:2, :] * keep + jnp.sum(w * by_row(SLOTS), axis=0, keepdims=True)
        total = num_t[...] * keep
        for i in range(NZ * NK // 4):
            for u in range(4):
                s = i * 4 + u
                weight[s * SLOTS : (s + 1) * SLOTS, :] = jnp.where(
                    slot_iota == rank[s : s + 1, :], w[s : s + 1, :], 0.0
                ).astype(BF16)
            values = jnp.concatenate([msg[base + i * 4 + u] for u in range(4)], axis=0)
            total = total + dot(values, weight[i * 4 * SLOTS : (i + 1) * 4 * SLOTS, :], 0, 0)
        num_t[...] = total
        return carry

    lax.fori_loop(0, 4, merge, 0)

    top, den = running[0:1, :], running[1:2, :]

    xmsg[x, 0:WIDTH, :] = num_t[...].astype(BF16)
    den_high = den.astype(BF16).astype(F32)
    xmsg[x, WIDTH : WIDTH + 16, :] = jnp.concatenate(
        [top, den_high, den - den_high, jnp.zeros((13, ROWS), F32)], axis=0
    ).astype(BF16)
    arrivals = []
    for j in range(1, NX):
        cp = remote(xmsg.at[x], xmsg.at[x], x_send.at[j - 1], x_recv.at[j - 1], c, (x + j) % NX)
        cp.start()
        arrivals.append(cp)
    pending += arrivals
    for cp in arrivals:
        cp.wait_recv()
    tails = [xmsg[i, WIDTH : WIDTH + 16, :].astype(F32) for i in range(NX)]
    best = functools.reduce(jnp.maximum, [v[0:1] for v in tails])
    num, den = 0.0, 0.0
    for i in range(NX):
        f = jnp.exp2(tails[i][0:1] - best)
        den = den + f * (tails[i][1:2] + tails[i][2:3])
        num = num + f * xmsg[i, 0:WIDTH, :].astype(F32)
    att_t[...] = (num / den).astype(BF16)

    def half(v_ref, which):
        return v_ref[:, pl.ds(pl.multiple_of(which * 128, 128), 128)]

    def reduce_scatter(n, piece, use):
        cores, along_y, along_z = [], [], []
        for h in range(2):
            core_out[n, h] = piece(1 - k, h).astype(BF16)
            cp = remote(core_out.at[n, h], core_in.at[n, h], c_send.at[n, h], c_recv.at[n, h], other, x)
            cp.start()
            cores.append(cp)
        for h in range(2):
            mine = piece(k, h)
            cores[h].wait_recv()
            total = mine + core_in[n, h].astype(F32)
            y_out[n, h] = total.reshape(NY, 32, HALF).astype(BF16)
            copies = []
            for j in range(1, NY):
                to = (y + j) % NY
                cp = remote(
                    y_out.at[n, h, to], y_in.at[n, h, j - 1], y_send.at[n, h, j - 1], y_recv.at[n, h, j - 1], ctx_of(to, z, k), x
                )
                cp.start()
                copies.append(cp)
            along_y.append(copies)
        for h in range(2):
            acc = y_out[n, h, y].astype(F32)
            for j, cp in enumerate(along_y[h]):
                cp.wait_recv()
                acc = acc + y_in[n, h, j].astype(F32)
            regroup(acc, z_out.at[n, h])
            copies = []
            for j in range(1, NZ):
                to = (z + j) % NZ
                cp = remote(
                    z_out.at[n, h, to], z_in.at[n, h, j - 1], z_send.at[n, h, j - 1], z_recv.at[n, h, j - 1], ctx_of(y, to, k), x
                )
                cp.start()
                copies.append(cp)
            along_z.append(copies)
        for h in range(2):
            acc = z_out[n, h, z].astype(F32)
            for j, cp in enumerate(along_z[h]):
                cp.wait_recv()
                acc = acc + z_in[n, h, j].astype(F32)
            use(h, acc)
        for copies in [cores] + along_y + along_z:
            pending.extend(copies)

    rows_z, rows_y, rows_c = [], [], []

    def spread(h, projected):
        stream = (fold(residual_ref[:, h * HALF : (h + 1) * HALF].astype(F32)) + projected).astype(BF16)
        z_all[h, z] = stream
        for j in range(1, NZ):
            cp = remote(z_all.at[h, z], z_all.at[h, z], gz_send.at[h, j - 1], gz_recv.at[h, j - 1], ctx_of(y, (z + j) % NZ, k), x)
            cp.start()
            rows_z.append(cp)
        unfold(stream.astype(F32), stream_ref, h)

    loads[0].wait()
    reduce_scatter(0, lambda which, h: dot(half(att_t, which), wo[:, h * HALF : (h + 1) * HALF], 0, 0), spread)
    for h in range(2):
        for cp in rows_z[h * (NZ - 1) : (h + 1) * (NZ - 1)]:
            cp.wait_recv()

        def put(b, v):
            x_all[h, k, y, :, b * 256 : (b + 1) * 256] = v

        ungroup(z_all.at[h], put)
        for j in range(1, NY):
            ref = x_all.at[h, k, y]
            cp = remote(ref, ref, gy_send.at[h, j - 1], gy_recv.at[h, j - 1], ctx_of((y + j) % NY, z, k), x)
            cp.start()
            rows_y.append(cp)

    def gate_up(which, h):
        wide = x_all[h, which].reshape(128, HALF).astype(F32)
        squares = jnp.sum(wide * wide, axis=1, keepdims=True)
        cut = slice(h * HALF, (h + 1) * HALF)
        scaled = (wide * gain_ref[:, cut]).astype(BF16)
        lane = lax.broadcasted_iota(jnp.int32, (128, 256 - UNITS), 1)
        parts = [dot(scaled, weight_ref[:, cut], 1, 1) for weight_ref in (wg, wu)]
        if h == 0:
            for n in range(2):
                gu32[n, which, :, 0:UNITS] = parts[n]
            gu32[0, which, :, UNITS:256] = jnp.where(lane < 2, squares, 0.0)
            gu32[1, which, :, UNITS:256] = jnp.zeros((128, 256 - UNITS), F32)
        else:
            for n in range(2):
                gu32[n, which, :, 0:UNITS] += parts[n]
            squares = squares + gu32[0, which, :, UNITS : UNITS + 1]
            high = squares.astype(BF16).astype(F32)
            gu32[0, which, :, UNITS:256] = jnp.where(lane == 0, high, squares - high)

    loads[1].wait()
    loads[2].wait()
    for h in range(2):
        for cp in rows_y[h * (NY - 1) : (h + 1) * (NY - 1)]:
            cp.wait_recv()
        cp = remote(x_all.at[h, k], x_all.at[h, k], gc_send.at[h], gc_recv.at[h], other, x)
        cp.start()
        rows_c.append(cp)
        gate_up(k, h)
    for h in range(2):
        rows_c[h].wait_recv()
        gate_up(1 - k, h)
    pending += rows_z + rows_y + rows_c

    for q in range(NX):
        for n in range(2):
            gu_out[q, n] = gu32[n, q // 2, (q % 2) * 64 : (q % 2) * 64 + 64, :].astype(BF16)
    arrivals = []
    for j in range(1, NX):
        to = (x + j) % NX
        cp = remote(gu_out.at[to], gu_in.at[j - 1], r_send.at[j - 1], r_recv.at[j - 1], c, to)
        cp.start()
        pending.append(cp)
        arrivals.append(cp)
    acc = gu_out[x].astype(F32)
    for j, cp in enumerate(arrivals):
        cp.wait_recv()
        acc = acc + gu_in[j].astype(F32)
    squares = acc[0, :, UNITS : UNITS + 1] + acc[0, :, UNITS + 1 : UNITS + 2]
    factor = lax.rsqrt(squares / MODEL + EPS)
    gate = acc[0] * factor
    up = acc[1] * factor
    lane = lax.broadcasted_iota(jnp.int32, (64, 256), 1)
    hidden = jnp.where(lane < UNITS, gate / (1.0 + jnp.exp(-gate)) * up, 0.0)
    hid[x] = hidden.astype(BF16)
    arrivals = []
    for j in range(1, NX):
        cp = remote(hid.at[x], hid.at[x], h_send.at[j - 1], h_recv.at[j - 1], c, (x + j) % NX)
        cp.start()
        pending.append(cp)
        arrivals.append(cp)
    for cp in arrivals:
        cp.wait_recv()
    loads[3].wait()

    def down(which, h):
        rows = hid[pl.ds(which * 2, 2)].reshape(128, 256)
        return dot(rows, wd[:, h * HALF : (h + 1) * HALF], 1, 0)

    reduce_scatter(1, down, lambda h, total: unfold(total, update_ref, h))
    for cp in pending:
        cp.wait_send()
    for j in range(1, 4):
        to = (y + j) % NY
        for first in (y % 2, 2 + to % 2):
            for i in range(4):
                src, send, recv = piece_of(first, 0, i, j)
                remote(src, src, send, recv, other, x).wait_send()
        for hp in ((y % 2 + 1) % 2, 2 + (to % 2 + 1) % 2):
            remote(block(hp, 0), block(hp, 0), p3_send.at[hp, j - 1], p3_recv.at[hp, j - 1], other, x).wait_send()
    for hp in range(4):
        for j in range(4):
            pass_on(hp, 0, j).wait_send()

    def sent(n, carry):
        @pl.when(n != c)
        def _():
            remote(sendbuf.at[n], msg.at[n], a_send.at[n], a_recv.at[n], n, x).wait_send()
            remote(tops_out.at[n], tops_in.at[n], b_send.at[n], b_recv.at[n], n, x).wait_send()

        return carry

    lax.fori_loop(0, CTX, sent, 0)

def swap4(v):
    return pltpu.roll(v, 4, 1)


def fold(v):
    return jnp.concatenate([v[:, b * 256 : (b + 1) * 256] for b in range(4)], axis=0)


def unfold(v, out_ref, h):
    for b in range(4):
        at = h * HALF + b * 256
        out_ref[:, at : at + 256] = v[4 * b : 4 * b + 4].astype(BF16)


def regroup(acc, out_ref):
    parts = [acc[:, b * 256 : (b + 1) * 256].reshape(4, 8, 256) for b in range(4)]
    lower = lax.broadcasted_iota(jnp.int32, (4, 8, 256), 1) < 4
    even = [jnp.where(lower, parts[b], swap4(parts[b + 1])) for b in (0, 2)]
    odd = [jnp.where(lower, swap4(parts[b]), parts[b + 1]) for b in (0, 2)]
    for t in range(4):
        out_ref[2 * t] = jnp.concatenate([even[0][t], even[1][t]], axis=0).astype(BF16)
        out_ref[2 * t + 1] = jnp.concatenate([odd[0][t], odd[1][t]], axis=0).astype(BF16)


def ungroup(src_ref, store):
    a = src_ref[...].astype(F32)
    lower = lax.broadcasted_iota(jnp.int32, (8, 256), 0) < 4
    columns = [[], [], [], []]
    for t in range(4):
        for q in range(2):
            e = a[2 * t, 8 * q : 8 * q + 8]
            o = a[2 * t + 1, 8 * q : 8 * q + 8]
            columns[2 * q].append(jnp.where(lower, e, pltpu.roll(o, 4, 0)))
            columns[2 * q + 1].append(jnp.where(lower, pltpu.roll(e, 4, 0), o))
    for b in range(4):
        store(b, jnp.concatenate(columns[b], axis=0).astype(BF16))


def hand_out(stream_in, update_in, stream_ref, update_ref):
    stream_ref[...] = stream_in[...]
    update_ref[...] = update_in[...]


def dma(*shape):
    return pltpu.SemaphoreType.DMA(shape)


def per_device(query, keys, values, chosen, residual, output_weight, norm_gain, gate_weight, up_weight, down_weight):
    vmem = pl.BlockSpec(memory_space=pltpu.VMEM)
    hbm = pl.BlockSpec(memory_space=pl.ANY)
    stream, update = pl.pallas_call(
        layer_kernel,
        out_shape=[jax.ShapeDtypeStruct((4, LOCAL), BF16)] * 2,
        in_specs=[hbm, hbm, vmem, hbm, hbm, hbm, hbm, hbm, hbm, hbm],
        out_specs=[vmem, vmem],
        scratch_shapes=[
            pltpu.VMEM((4, 16, WIDTH), BF16),
            pltpu.VMEM((HEADS, 16, ROWS), jnp.int32),
            pltpu.VMEM((1, LOCAL), F32),
            pltpu.VMEM((4, ROWS, 16, WIDTH), BF16),
            pltpu.VMEM((ROWS, 16, WIDTH), BF16),
            pltpu.VMEM((HEADS, KEYS, WIDTH), BF16),
            pltpu.VMEM((HEADS, KEYS, WIDTH), BF16),
            pltpu.VMEM((SLOTS * GROUP, WIDTH), F32),
            pltpu.VMEM((SLOTS * GROUP, WIDTH), F32),
            pltpu.VMEM((SLOTS * GROUP, WIDTH), F32),
            pltpu.VMEM((CTX, SLOTS, WIDTH), BF16),
            pltpu.VMEM((CTX, SLOTS, WIDTH), BF16),
            pltpu.VMEM((CTX, 1, WIDTH), F32),
            pltpu.VMEM((CTX, 1, WIDTH), F32),
            pltpu.VMEM((HEADS * 16, ROWS), F32),
            pltpu.VMEM((HEADS, ROWS), F32),
            pltpu.VMEM((CTX, ROWS), F32),
            pltpu.VMEM((HEADS, 128), jnp.int32),
            pltpu.SMEM((HEADS, 128), jnp.int32),
            pltpu.VMEM((WIDTH, LOCAL), BF16),
            pltpu.VMEM((UNITS, LOCAL), BF16),
            pltpu.VMEM((UNITS, LOCAL), BF16),
            pltpu.VMEM((256, LOCAL), BF16),
            pltpu.VMEM((16 * SLOTS, ROWS), BF16),
            pltpu.VMEM((16, WIDTH), F32),
            pltpu.VMEM((8, ROWS), F32),
            pltpu.VMEM((WIDTH, ROWS), F32),
            pltpu.VMEM((NX, WIDTH + 16, ROWS), BF16),
            pltpu.VMEM((WIDTH, ROWS), BF16),
            pltpu.VMEM((2, 2, 128, HALF), BF16),
            pltpu.VMEM((2, 2, 128, HALF), BF16),
            pltpu.VMEM((2, 2, NY, 32, HALF), BF16),
            pltpu.VMEM((2, 2, NY - 1, 32, HALF), BF16),
            pltpu.VMEM((2, 2, NZ, 16, 256), BF16),
            pltpu.VMEM((2, 2, NZ - 1, 16, 256), BF16),
            pltpu.VMEM((2, NZ, 16, 256), BF16),
            pltpu.VMEM((2, NK, NY, 32, HALF), BF16),
            pltpu.VMEM((2, NK, 128, 256), F32),
            pltpu.VMEM((NX, 2, 64, 256), BF16),
            pltpu.VMEM((NX - 1, 2, 64, 256), BF16),
            pltpu.VMEM((NX, 64, 256), BF16),
            dma(HEADS), dma(HEADS), pltpu.SemaphoreType.DMA,
            dma(2, 7), dma(2, 7), dma(2, 3), dma(2, 3), dma(4, 3), dma(4, 3), dma(4, 3, 4), dma(4, 3, 4), dma(4, 4), dma(4, 4),
            dma(CTX), dma(CTX), dma(CTX), dma(CTX), dma(3),
            dma(4), dma(3), dma(3),
            dma(2, 2), dma(2, 2), dma(2, 2, 3), dma(2, 2, 3), dma(2, 2, 7), dma(2, 2, 7),
            dma(2, 7), dma(2, 7), dma(2, 3), dma(2, 3), dma(2), dma(2),
            dma(3), dma(3), dma(3), dma(3),
        ],
        compiler_params=pltpu.CompilerParams(collective_id=0, has_side_effects=True, vmem_limit_bytes=VMEM_LIMIT),
        name="layer",
    )(
        query.reshape(4, 16, WIDTH), chosen.transpose(0, 2, 1), residual, norm_gain.reshape(1, LOCAL),
        keys[0], values[0], output_weight, gate_weight.T, up_weight.T, down_weight,
    )
    return pl.pallas_call(
        hand_out,
        out_shape=[jax.ShapeDtypeStruct((4, LOCAL), BF16)] * 2,
        in_specs=[vmem, vmem],
        out_specs=[vmem, vmem],
        name="hand_out",
    )(stream, update)


def solution(mesh):
    return jax.shard_map(
        per_device,
        mesh=mesh,
        in_specs=(
            P(("ctx", "mp"), None, None, None),
            P(("ctx", "mp"), None, None, None),
            P(("ctx", "mp"), None, None, None),
            P(),
            P("ctx", "mp"),
            P("ctx", "mp"),
            P("mp"),
            P("mp", "ctx"),
            P("mp", "ctx"),
            P("ctx", "mp"),
        ),
        out_specs=(P("ctx", "mp"), P("ctx", "mp")),
        check_vma=False,
    )
```

```python
import functools
import math

import jax
import jax.numpy as jnp
from jax import lax
from jax.experimental import pallas as pl
from jax.experimental.pallas import tpu as pltpu
from jax.sharding import PartitionSpec as P

NX, NY, NZ, NK = 4, 4, 8, 2
CTX = NY * NZ * NK
ROWS, HEADS, GROUP, WIDTH = 256, 8, 8, 128
KEYS, SLOTS = 2048, 64
MODEL, LOCAL, HALF, UNITS = 8192, 2048, 1024, 224
EPS = 1e-5
LOWEST = -1e30
SCALE = WIDTH**-0.5 * math.log2(math.e)
MESH = pl.DeviceIdType.MESH
VMEM_LIMIT = 56 * 1024 * 1024
F32, BF16 = jnp.float32, jnp.bfloat16


def place():
    c = lax.axis_index("ctx")
    x = lax.axis_index("mp")
    return c, x, c // (NZ * NK), (c // NK) % NZ, c % NK


def ctx_of(y, z, k):
    return (y * NZ + z) * NK + k


def remote(src, dst, send_sem, recv_sem, ctx, mp):
    return pltpu.make_async_remote_copy(
        src_ref=src,
        dst_ref=dst,
        send_sem=send_sem,
        recv_sem=recv_sem,
        device_id=(ctx, mp),
        device_id_type=MESH,
    )


def dot(a, b, da, db):
    return lax.dot_general(a, b, (((da,), (db,)), ((), ())), preferred_element_type=F32)


def hp_at(t, y):
    return ((y // 2 + t % 2) % 2) * 2 + (y % 2 + t // 2) % 2


def layer_kernel(
    own_hbm, chosen_hbm, residual_ref, gain_hbm, keys_ref, values_ref, wo_hbm, wg_hbm, wu_hbm, wd_hbm,
    stream_ref, update_ref,
    own_ref, chosen_ref, gain_ref, qbuf, qpair, kbuf, vbuf, q32, o32, st32, sendbuf, msg, tops_out, tops_in, picked, ranks, plane, slots_vmem, slots,
    wo, wg, wu, wd, weight, stats, running, num_t, xmsg, att_t,
    core_out, core_in, y_out, y_in, z_out, z_in,
    z_all, x_all, gu32, gu_out, gu_in, hid,
    k_sem, v_sem, s_sem,
    qz_send, qz_recv, p2_send, p2_recv, p3_send, p3_recv, p4_send, p4_recv, qc_send, qc_recv,
    a_send, a_recv, b_send, b_recv, i_sem,
    w_sem, x_send, x_recv,
    c_send, c_recv, y_send, y_recv, z_send, z_recv,
    gz_send, gz_recv, gy_send, gy_recv, gc_send, gc_recv,
    r_send, r_recv, h_send, h_recv,
):
    c, x, y, z, k = place()
    other = ctx_of(y, z, 1 - k)
    pending = []

    barrier = pltpu.get_barrier_semaphore()
    pl.semaphore_signal(barrier, inc=1, device_id=(other, x), device_id_type=MESH)
    for j in range(1, NX):
        pl.semaphore_signal(barrier, inc=1, device_id=(c, (x + j) % NX), device_id_type=MESH)
    for j in range(1, NY):
        pl.semaphore_signal(barrier, inc=1, device_id=(ctx_of((y + j) % NY, z, k), x), device_id_type=MESH)
    for j in range(1, NZ):
        pl.semaphore_signal(barrier, inc=1, device_id=(ctx_of(y, (z + j) % NZ, k), x), device_id_type=MESH)

    def load(t, carry):
        h = hp_at(t // 2, y) * 2 + t % 2
        pltpu.make_async_copy(keys_ref.at[h], kbuf.at[h], k_sem.at[h]).start()
        pltpu.make_async_copy(values_ref.at[h], vbuf.at[h], v_sem.at[h]).start()
        return carry

    row_a = ((k * NX + x) * NY + y) * NZ
    row_b = ((k * NY + y) * NX + x) * NZ
    given = [
        pltpu.make_async_copy(own_hbm, own_ref, i_sem.at[0]),
        pltpu.make_async_copy(chosen_hbm, chosen_ref, i_sem.at[1]),
        pltpu.make_async_copy(gain_hbm, gain_ref, i_sem.at[2]),
    ]
    for cp in given:
        cp.start()
    given[0].wait()
    qbuf[0:2, row_a + z] = own_ref[0:2]
    qbuf[2:4, row_b + z] = own_ref[2:4]
    pl.semaphore_wait(barrier, 1 + NX - 1 + NY - 1 + NZ - 1)

    arrivals = []
    for j in range(1, NZ):
        to = ctx_of(y, (z + j) % NZ, k)
        for half, row in ((0, row_a), (1, row_b)):
            ref = qbuf.at[pl.ds(2 * half, 2), row + z]
            cp = remote(ref, ref, qz_send.at[half, j - 1], qz_recv.at[half, j - 1], to, x)
            cp.start()
            arrivals.append(cp)
    pending += arrivals
    lax.fori_loop(0, HEADS, load, 0)

    loads = [
        pltpu.make_async_copy(wo_hbm, wo, w_sem.at[0]),
        pltpu.make_async_copy(wg_hbm, wg, w_sem.at[1]),
        pltpu.make_async_copy(wu_hbm, wu, w_sem.at[2]),
        pltpu.make_async_copy(wd_hbm, wd.at[pl.ds(0, UNITS)], w_sem.at[3]),
    ]
    for cp in loads:
        cp.start()
    wd[UNITS:256, :] = jnp.zeros((256 - UNITS, LOCAL), BF16)

    for cp in given[1:]:
        cp.wait()

    r_in = lax.broadcasted_iota(jnp.int32, (ROWS, ROWS), 0)
    r_out = lax.broadcasted_iota(jnp.int32, (ROWS, ROWS), 1)
    moved = ((r_in // 64) * 32 + ((r_in // 8) % 8) * 4 + r_in % 4) + ((r_in // 4) % 2) * 128
    permute = jnp.where(moved == r_out, 1.0, 0.0).astype(BF16)
    before = jnp.where(r_in < r_out, 1.0, 0.0).astype(BF16)
    listed = chosen_ref[...].reshape(HEADS * 16, ROWS).astype(F32).astype(BF16)
    picked[...] = dot(listed, permute, 1, 0)
    own_id = (c * NX + x).astype(F32)
    found = [
        jnp.max(jnp.where(picked[h * 16 : h * 16 + 16, :] == own_id, 1.0, 0.0), axis=0, keepdims=True)
        for h in range(HEADS)
    ]
    member = jnp.concatenate(found, axis=0)
    ranks[...] = jnp.where(member > 0.5, dot(jnp.concatenate([member, member], axis=0).astype(BF16), before, 1, 0)[0:HEADS], -1.0)
    ids = (lax.broadcasted_iota(jnp.int32, (CTX, ROWS), 0) * NX + x).astype(F32)
    member = jnp.zeros((CTX, ROWS), F32)
    for i in range(16):
        row = picked[pl.ds((c // GROUP) * 16 + i, 1), :]
        member = jnp.maximum(member, jnp.where(row == ids, 1.0, 0.0))
    plane[...] = jnp.where(member > 0.5, dot(member.astype(BF16), before, 1, 0), -1.0)
    r8 = lax.broadcasted_iota(jnp.int32, (16, ROWS), 1)
    kk, yy, zz, mm = r8 // 128, (r8 // 32) % 4, (r8 // 4) % 8, r8 % 4
    pos_a = (((kk * NX + mm) * NY + yy) * NZ + zz).astype(F32).astype(BF16)
    pos_b = (((kk * NY + yy) * NX + mm) * NZ + zz).astype(F32).astype(BF16)
    spot = lax.broadcasted_iota(jnp.int32, (128, ROWS), 0).astype(F32)
    for h in range(HEADS):
        hit = jnp.where(spot == ranks[h : h + 1, :], 1.0, 0.0).astype(BF16)
        at = dot(pos_a if h < 4 else pos_b, hit, 1, 1)
        slots_vmem[h : h + 1, :] = at[0:1].astype(jnp.int32)
    to_scalar = pltpu.make_async_copy(slots_vmem, slots, s_sem)
    to_scalar.start()
    for cp in arrivals:
        cp.wait_recv()

    arrivals = []
    for j in range(1, 4):
        ref = qbuf.at[0:2, pl.ds(row_a, NZ)]
        cp = remote(ref, ref, p2_send.at[0, j - 1], p2_recv.at[0, j - 1], ctx_of((y + j) % NY, z, k), x)
        cp.start()
        arrivals.append(cp)
        ref = qbuf.at[2:4, pl.ds(row_b, NZ)]
        cp = remote(ref, ref, p2_send.at[1, j - 1], p2_recv.at[1, j - 1], c, (x + j) % NX)
        cp.start()
        arrivals.append(cp)
    pending += arrivals

    def block(hp, n):
        return qbuf.at[hp, pl.ds(n * 32, 32)]

    def pass_on(hp, n, j):
        return remote(block(hp, n), block(hp, n), qc_send.at[hp, j], qc_recv.at[hp, j], other, x)

    def piece_of(hp, row, i, j):
        ref = qbuf.at[hp, pl.ds(row, NZ)]
        return ref, p4_send.at[hp, j - 1, i], p4_recv.at[hp, j - 1, i]

    for i in range(4):
        if i:
            for cp in arrivals[2 * i - 2 : 2 * i]:
                cp.wait_recv()
        for j in range(1, 4):
            ref, send, recv = piece_of(y % 2, ((k * NX + x) * NY + (y - i + NY) % NY) * NZ, i, j)
            remote(ref, ref, send, recv, c, (x + j) % NX).start()
            to = (y + j) % NY
            ref, send, recv = piece_of(2 + to % 2, ((k * NY + y) * NX + (x - i + NX) % NX) * NZ, i, j)
            remote(ref, ref, send, recv, ctx_of(to, z, k), x).start()
    for j in range(1, 4):
        hp = (y % 2 + 1) % 2
        ref = block(hp, k * NX + x)
        remote(ref, ref, p3_send.at[hp, j - 1], p3_recv.at[hp, j - 1], c, (x + j) % NX).start()
        to = (y + j) % NY
        hp = 2 + (to % 2 + 1) % 2
        ref = block(hp, k * NY + y)
        remote(ref, ref, p3_send.at[hp, j - 1], p3_recv.at[hp, j - 1], ctx_of(to, z, k), x).start()
    for hp in range(4):
        pass_on(hp, k * 4 + (x if hp < 2 else y), 0).start()

    def forward(hp, pieces):
        late = hp // 2
        for j in range(1, 4):
            n = k * 4 + (x * (1 - late) + y * late - j + 4) % 4
            ref = block(hp, n)
            if pieces:
                for i in range(4):
                    src, send, recv = piece_of(hp, n * 32, i, j)
                    remote(src, src, send, recv, other, x).wait_recv()
            else:
                remote(ref, ref, p3_send.at[hp, j - 1], p3_recv.at[hp, j - 1], other, x).wait_recv()
            pass_on(hp, n, j).start()

    forward(hp_at(0, y), True)
    forward(hp_at(1, y), True)
    to_scalar.wait()
    slot_iota = lax.broadcasted_iota(jnp.int32, (SLOTS, ROWS), 0).astype(F32)

    def head(h):
        hp = h // 2
        upper = (h % 2) == 1
        pltpu.make_async_copy(keys_ref.at[h], kbuf.at[h], k_sem.at[h]).wait()
        pltpu.make_async_copy(values_ref.at[h], vbuf.at[h], v_sem.at[h]).wait()

        def pick(i, carry):
            for u in range(8):
                s = i * 8 + u
                row = jnp.minimum(jnp.maximum(slots[h, s], 0), ROWS - 1)
                tile = qpair[row].astype(F32)
                q32[pl.ds(pl.multiple_of(s * 8, 8), 8), :] = jnp.where(upper, tile[8:16], tile[0:8])
            return carry

        lax.fori_loop(0, SLOTS // 8, pick, 0)

        for b in range(4):
            at = pl.ds(b * 128, 128)
            s = dot(q32[at, :].astype(BF16), kbuf[h], 1, 1)
            top = (jnp.max(s, axis=1, keepdims=True) * SCALE).astype(BF16).astype(F32)
            p = jnp.exp2(s * SCALE - top)
            total = jnp.sum(p, axis=1, keepdims=True)
            o32[at, :] = dot(p.astype(BF16), vbuf[h], 1, 0)
            lane = lax.broadcasted_iota(jnp.int32, (128, WIDTH), 1)
            st32[at, :] = jnp.where(lane == 0, top, total)

        lane = lax.broadcasted_iota(jnp.int32, (SLOTS, WIDTH), 1)
        slot = lax.broadcasted_iota(jnp.int32, (SLOTS, WIDTH), 0)
        for g in range(GROUP):
            n = h * GROUP + g
            sendbuf[n] = o32[pl.ds(g, SLOTS, stride=GROUP), :].astype(BF16)
            st = st32[pl.ds(g, SLOTS, stride=GROUP), :]
            spread = jnp.where(lane == slot, st[:, 0:1], jnp.where(lane == slot + SLOTS, st[:, 1:2], 0.0))
            tops_out[n] = jnp.sum(spread, axis=0, keepdims=True)

            @pl.when(n != c)
            def _():
                remote(sendbuf.at[n], msg.at[c], a_send.at[n], a_recv.at[c], n, x).start()
                remote(tops_out.at[n], tops_in.at[c], b_send.at[n], b_recv.at[c], n, x).start()

            @pl.when(n == c)
            def _():
                msg[c] = sendbuf[n]
                tops_in[c] = tops_out[n]

    def pair(t, carry):
        hp = hp_at(t, y)
        for j in range(4):
            pass_on(hp, 0, j).wait_recv()
        qpair[...] = qbuf[hp]
        lax.fori_loop(0, 2, lambda i, v: (head(hp * 2 + i), v)[1], 0)

        @pl.when(t < 2)
        def _():
            forward(hp_at(t + 2, y), False)

        return carry

    lax.fori_loop(0, 4, pair, 0)

    num_t[...] = jnp.zeros_like(num_t)
    running[0:1, :] = jnp.full((1, ROWS), LOWEST, F32)
    running[1:2, :] = jnp.zeros((1, ROWS), F32)

    def merge(t, carry):
        base = hp_at(t, y) * (NZ * NK)

        def arrive(i, v):
            s = base + i

            @pl.when(s != c)
            def _():
                remote(sendbuf.at[s], msg.at[s], a_send.at[s], a_recv.at[s], s, x).wait_recv()
                remote(tops_out.at[s], tops_in.at[s], b_send.at[s], b_recv.at[s], s, x).wait_recv()

            return v

        lax.fori_loop(0, NZ * NK, arrive, 0)
        for i in range(NZ * NK):
            stats[i : i + 1, :] = tops_in[base + i]
        held = stats[...]
        rank = plane[pl.ds(pl.multiple_of(base, 16), 16), :]
        at = jnp.maximum(rank, 0.0).astype(jnp.int32)

        def by_row(first):
            return jnp.concatenate(
                [
                    jnp.take_along_axis(held, at[:, i * 128 : (i + 1) * 128] + first, axis=1, mode="promise_in_bounds")
                    for i in range(2)
                ],
                axis=1,
            )

        listed = rank >= 0.0
        top_each = jnp.where(listed, by_row(0), LOWEST)
        old = running[0:1, :]
        top = jnp.maximum(old, jnp.max(top_each, axis=0, keepdims=True))
        keep = jnp.exp2(old - top)
        w = jnp.where(listed, jnp.exp2(top_each - top), 0.0).astype(BF16).astype(F32)
        running[0:1, :] = top
        running[1:2, :] = running[1:2, :] * keep + jnp.sum(w * by_row(SLOTS), axis=0, keepdims=True)
        total = num_t[...] * keep
        for i in range(NZ * NK // 4):
            for u in range(4):
                s = i * 4 + u
                weight[s * SLOTS : (s + 1) * SLOTS, :] = jnp.where(
                    slot_iota == rank[s : s + 1, :], w[s : s + 1, :], 0.0
                ).astype(BF16)
            values = jnp.concatenate([msg[base + i * 4 + u] for u in range(4)], axis=0)
            total = total + dot(values, weight[i * 4 * SLOTS : (i + 1) * 4 * SLOTS, :], 0, 0)
        num_t[...] = total
        return carry

    lax.fori_loop(0, 4, merge, 0)

    top, den = running[0:1, :], running[1:2, :]

    xmsg[x, 0:WIDTH, :] = num_t[...].astype(BF16)
    den_high = den.astype(BF16).astype(F32)
    xmsg[x, WIDTH : WIDTH + 16, :] = jnp.concatenate(
        [top, den_high, den - den_high, jnp.zeros((13, ROWS), F32)], axis=0
    ).astype(BF16)
    arrivals = []
    for j in range(1, NX):
        cp = remote(xmsg.at[x], xmsg.at[x], x_send.at[j - 1], x_recv.at[j - 1], c, (x + j) % NX)
        cp.start()
        arrivals.append(cp)
    pending += arrivals
    for cp in arrivals:
        cp.wait_recv()
    tails = [xmsg[i, WIDTH : WIDTH + 16, :].astype(F32) for i in range(NX)]
    best = functools.reduce(jnp.maximum, [v[0:1] for v in tails])
    num, den = 0.0, 0.0
    for i in range(NX):
        f = jnp.exp2(tails[i][0:1] - best)
        den = den + f * (tails[i][1:2] + tails[i][2:3])
        num = num + f * xmsg[i, 0:WIDTH, :].astype(F32)
    att_t[...] = (num / den).astype(BF16)

    def half(v_ref, which):
        return v_ref[:, pl.ds(pl.multiple_of(which * 128, 128), 128)]

    def reduce_scatter(n, piece, use):
        cores, along_y, along_z = [], [], []
        for h in range(2):
            core_out[n, h] = piece(1 - k, h).astype(BF16)
            cp = remote(core_out.at[n, h], core_in.at[n, h], c_send.at[n, h], c_recv.at[n, h], other, x)
            cp.start()
            cores.append(cp)
        for h in range(2):
            mine = piece(k, h)
            cores[h].wait_recv()
            total = mine + core_in[n, h].astype(F32)
            y_out[n, h] = total.reshape(NY, 32, HALF).astype(BF16)
            copies = []
            for j in range(1, NY):
                to = (y + j) % NY
                cp = remote(
                    y_out.at[n, h, to], y_in.at[n, h, j - 1], y_send.at[n, h, j - 1], y_recv.at[n, h, j - 1], ctx_of(to, z, k), x
                )
                cp.start()
                copies.append(cp)
            along_y.append(copies)
        for h in range(2):
            acc = y_out[n, h, y].astype(F32)
            for j, cp in enumerate(along_y[h]):
                cp.wait_recv()
                acc = acc + y_in[n, h, j].astype(F32)
            regroup(acc, z_out.at[n, h])
            copies = []
            for j in range(1, NZ):
                to = (z + j) % NZ
                cp = remote(
                    z_out.at[n, h, to], z_in.at[n, h, j - 1], z_send.at[n, h, j - 1], z_recv.at[n, h, j - 1], ctx_of(y, to, k), x
                )
                cp.start()
                copies.append(cp)
            along_z.append(copies)
        for h in range(2):
            acc = z_out[n, h, z].astype(F32)
            for j, cp in enumerate(along_z[h]):
                cp.wait_recv()
                acc = acc + z_in[n, h, j].astype(F32)
            use(h, acc)
        for copies in [cores] + along_y + along_z:
            pending.extend(copies)

    rows_z, rows_y, rows_c = [], [], []

    def spread(h, projected):
        stream = (fold(residual_ref[:, h * HALF : (h + 1) * HALF].astype(F32)) + projected).astype(BF16)
        z_all[h, z] = stream
        for j in range(1, NZ):
            cp = remote(z_all.at[h, z], z_all.at[h, z], gz_send.at[h, j - 1], gz_recv.at[h, j - 1], ctx_of(y, (z + j) % NZ, k), x)
            cp.start()
            rows_z.append(cp)
        unfold(stream.astype(F32), stream_ref, h)

    loads[0].wait()
    reduce_scatter(0, lambda which, h: dot(half(att_t, which), wo[:, h * HALF : (h + 1) * HALF], 0, 0), spread)
    for h in range(2):
        for cp in rows_z[h * (NZ - 1) : (h + 1) * (NZ - 1)]:
            cp.wait_recv()

        def put(b, v):
            x_all[h, k, y, :, b * 256 : (b + 1) * 256] = v

        ungroup(z_all.at[h], put)
        for j in range(1, NY):
            ref = x_all.at[h, k, y]
            cp = remote(ref, ref, gy_send.at[h, j - 1], gy_recv.at[h, j - 1], ctx_of((y + j) % NY, z, k), x)
            cp.start()
            rows_y.append(cp)

    def gate_up(which, h):
        wide = x_all[h, which].reshape(128, HALF).astype(F32)
        squares = jnp.sum(wide * wide, axis=1, keepdims=True)
        cut = slice(h * HALF, (h + 1) * HALF)
        scaled = (wide * gain_ref[:, cut]).astype(BF16)
        lane = lax.broadcasted_iota(jnp.int32, (128, 256 - UNITS), 1)
        parts = [dot(scaled, weight_ref[:, cut], 1, 1) for weight_ref in (wg, wu)]
        if h == 0:
            for n in range(2):
                gu32[n, which, :, 0:UNITS] = parts[n]
            gu32[0, which, :, UNITS:256] = jnp.where(lane < 2, squares, 0.0)
            gu32[1, which, :, UNITS:256] = jnp.zeros((128, 256 - UNITS), F32)
        else:
            for n in range(2):
                gu32[n, which, :, 0:UNITS] += parts[n]
            squares = squares + gu32[0, which, :, UNITS : UNITS + 1]
            high = squares.astype(BF16).astype(F32)
            gu32[0, which, :, UNITS:256] = jnp.where(lane == 0, high, squares - high)

    loads[1].wait()
    loads[2].wait()
    for h in range(2):
        for cp in rows_y[h * (NY - 1) : (h + 1) * (NY - 1)]:
            cp.wait_recv()
        cp = remote(x_all.at[h, k], x_all.at[h, k], gc_send.at[h], gc_recv.at[h], other, x)
        cp.start()
        rows_c.append(cp)
        gate_up(k, h)
    for h in range(2):
        rows_c[h].wait_recv()
        gate_up(1 - k, h)
    pending += rows_z + rows_y + rows_c

    for q in range(NX):
        for n in range(2):
            gu_out[q, n] = gu32[n, q // 2, (q % 2) * 64 : (q % 2) * 64 + 64, :].astype(BF16)
    arrivals = []
    for j in range(1, NX):
        to = (x + j) % NX
        cp = remote(gu_out.at[to], gu_in.at[j - 1], r_send.at[j - 1], r_recv.at[j - 1], c, to)
        cp.start()
        pending.append(cp)
        arrivals.append(cp)
    acc = gu_out[x].astype(F32)
    for j, cp in enumerate(arrivals):
        cp.wait_recv()
        acc = acc + gu_in[j].astype(F32)
    squares = acc[0, :, UNITS : UNITS + 1] + acc[0, :, UNITS + 1 : UNITS + 2]
    factor = lax.rsqrt(squares / MODEL + EPS)
    gate = acc[0] * factor
    up = acc[1] * factor
    lane = lax.broadcasted_iota(jnp.int32, (64, 256), 1)
    hidden = jnp.where(lane < UNITS, gate / (1.0 + jnp.exp(-gate)) * up, 0.0)
    hid[x] = hidden.astype(BF16)
    arrivals = []
    for j in range(1, NX):
        cp = remote(hid.at[x], hid.at[x], h_send.at[j - 1], h_recv.at[j - 1], c, (x + j) % NX)
        cp.start()
        pending.append(cp)
        arrivals.append(cp)
    for cp in arrivals:
        cp.wait_recv()
    loads[3].wait()

    def down(which, h):
        rows = hid[pl.ds(which * 2, 2)].reshape(128, 256)
        return dot(rows, wd[:, h * HALF : (h + 1) * HALF], 1, 0)

    reduce_scatter(1, down, lambda h, total: unfold(total, update_ref, h))
    for cp in pending:
        cp.wait_send()
    for j in range(1, 4):
        to = (y + j) % NY
        for first in (y % 2, 2 + to % 2):
            for i in range(4):
                src, send, recv = piece_of(first, 0, i, j)
                remote(src, src, send, recv, other, x).wait_send()
        for hp in ((y % 2 + 1) % 2, 2 + (to % 2 + 1) % 2):
            remote(block(hp, 0), block(hp, 0), p3_send.at[hp, j - 1], p3_recv.at[hp, j - 1], other, x).wait_send()
    for hp in range(4):
        for j in range(4):
            pass_on(hp, 0, j).wait_send()

    def sent(n, carry):
        @pl.when(n != c)
        def _():
            remote(sendbuf.at[n], msg.at[n], a_send.at[n], a_recv.at[n], n, x).wait_send()
            remote(tops_out.at[n], tops_in.at[n], b_send.at[n], b_recv.at[n], n, x).wait_send()

        return carry

    lax.fori_loop(0, CTX, sent, 0)

def swap4(v):
    return pltpu.roll(v, 4, 1)


def fold(v):
    return jnp.concatenate([v[:, b * 256 : (b + 1) * 256] for b in range(4)], axis=0)


def unfold(v, out_ref, h):
    for b in range(4):
        at = h * HALF + b * 256
        out_ref[:, at : at + 256] = v[4 * b : 4 * b + 4].astype(BF16)


def regroup(acc, out_ref):
    parts = [acc[:, b * 256 : (b + 1) * 256].reshape(4, 8, 256) for b in range(4)]
    lower = lax.broadcasted_iota(jnp.int32, (4, 8, 256), 1) < 4
    even = [jnp.where(lower, parts[b], swap4(parts[b + 1])) for b in (0, 2)]
    odd = [jnp.where(lower, swap4(parts[b]), parts[b + 1]) for b in (0, 2)]
    for t in range(4):
        out_ref[2 * t] = jnp.concatenate([even[0][t], even[1][t]], axis=0).astype(BF16)
        out_ref[2 * t + 1] = jnp.concatenate([odd[0][t], odd[1][t]], axis=0).astype(BF16)


def ungroup(src_ref, store):
    a = src_ref[...].astype(F32)
    lower = lax.broadcasted_iota(jnp.int32, (8, 256), 0) < 4
    columns = [[], [], [], []]
    for t in range(4):
        for q in range(2):
            e = a[2 * t, 8 * q : 8 * q + 8]
            o = a[2 * t + 1, 8 * q : 8 * q + 8]
            columns[2 * q].append(jnp.where(lower, e, pltpu.roll(o, 4, 0)))
            columns[2 * q + 1].append(jnp.where(lower, pltpu.roll(e, 4, 0), o))
    for b in range(4):
        store(b, jnp.concatenate(columns[b], axis=0).astype(BF16))


def hand_out(stream_in, update_in, stream_ref, update_ref):
    stream_ref[...] = stream_in[...]
    update_ref[...] = update_in[...]


def dma(*shape):
    return pltpu.SemaphoreType.DMA(shape)


def per_device(query, keys, values, chosen, residual, output_weight, norm_gain, gate_weight, up_weight, down_weight):
    vmem = pl.BlockSpec(memory_space=pltpu.VMEM)
    hbm = pl.BlockSpec(memory_space=pl.ANY)
    stream, update = pl.pallas_call(
        layer_kernel,
        out_shape=[jax.ShapeDtypeStruct((4, LOCAL), BF16)] * 2,
        in_specs=[hbm, hbm, vmem, hbm, hbm, hbm, hbm, hbm, hbm, hbm],
        out_specs=[vmem, vmem],
        scratch_shapes=[
            pltpu.VMEM((4, 16, WIDTH), BF16),
            pltpu.VMEM((HEADS, 16, ROWS), jnp.int32),
            pltpu.VMEM((1, LOCAL), F32),
            pltpu.VMEM((4, ROWS, 16, WIDTH), BF16),
            pltpu.VMEM((ROWS, 16, WIDTH), BF16),
            pltpu.VMEM((HEADS, KEYS, WIDTH), BF16),
            pltpu.VMEM((HEADS, KEYS, WIDTH), BF16),
            pltpu.VMEM((SLOTS * GROUP, WIDTH), F32),
            pltpu.VMEM((SLOTS * GROUP, WIDTH), F32),
            pltpu.VMEM((SLOTS * GROUP, WIDTH), F32),
            pltpu.VMEM((CTX, SLOTS, WIDTH), BF16),
            pltpu.VMEM((CTX, SLOTS, WIDTH), BF16),
            pltpu.VMEM((CTX, 1, WIDTH), F32),
            pltpu.VMEM((CTX, 1, WIDTH), F32),
            pltpu.VMEM((HEADS * 16, ROWS), F32),
            pltpu.VMEM((HEADS, ROWS), F32),
            pltpu.VMEM((CTX, ROWS), F32),
            pltpu.VMEM((HEADS, 128), jnp.int32),
            pltpu.SMEM((HEADS, 128), jnp.int32),
            pltpu.VMEM((WIDTH, LOCAL), BF16),
            pltpu.VMEM((UNITS, LOCAL), BF16),
            pltpu.VMEM((UNITS, LOCAL), BF16),
            pltpu.VMEM((256, LOCAL), BF16),
            pltpu.VMEM((16 * SLOTS, ROWS), BF16),
            pltpu.VMEM((16, WIDTH), F32),
            pltpu.VMEM((8, ROWS), F32),
            pltpu.VMEM((WIDTH, ROWS), F32),
            pltpu.VMEM((NX, WIDTH + 16, ROWS), BF16),
            pltpu.VMEM((WIDTH, ROWS), BF16),
            pltpu.VMEM((2, 2, 128, HALF), BF16),
            pltpu.VMEM((2, 2, 128, HALF), BF16),
            pltpu.VMEM((2, 2, NY, 32, HALF), BF16),
            pltpu.VMEM((2, 2, NY - 1, 32, HALF), BF16),
            pltpu.VMEM((2, 2, NZ, 16, 256), BF16),
            pltpu.VMEM((2, 2, NZ - 1, 16, 256), BF16),
            pltpu.VMEM((2, NZ, 16, 256), BF16),
            pltpu.VMEM((2, NK, NY, 32, HALF), BF16),
            pltpu.VMEM((2, NK, 128, 256), F32),
            pltpu.VMEM((NX, 2, 64, 256), BF16),
            pltpu.VMEM((NX - 1, 2, 64, 256), BF16),
            pltpu.VMEM((NX, 64, 256), BF16),
            dma(HEADS), dma(HEADS), pltpu.SemaphoreType.DMA,
            dma(2, 7), dma(2, 7), dma(2, 3), dma(2, 3), dma(4, 3), dma(4, 3), dma(4, 3, 4), dma(4, 3, 4), dma(4, 4), dma(4, 4),
            dma(CTX), dma(CTX), dma(CTX), dma(CTX), dma(3),
            dma(4), dma(3), dma(3),
            dma(2, 2), dma(2, 2), dma(2, 2, 3), dma(2, 2, 3), dma(2, 2, 7), dma(2, 2, 7),
            dma(2, 7), dma(2, 7), dma(2, 3), dma(2, 3), dma(2), dma(2),
            dma(3), dma(3), dma(3), dma(3),
        ],
        compiler_params=pltpu.CompilerParams(collective_id=0, has_side_effects=True, vmem_limit_bytes=VMEM_LIMIT),
        name="layer",
    )(
        query.reshape(4, 16, WIDTH), chosen.transpose(0, 2, 1), residual, norm_gain.reshape(1, LOCAL),
        keys[0], values[0], output_weight, gate_weight.T, up_weight.T, down_weight,
    )
    return pl.pallas_call(
        hand_out,
        out_shape=[jax.ShapeDtypeStruct((4, LOCAL), BF16)] * 2,
        in_specs=[vmem, vmem],
        out_specs=[vmem, vmem],
        name="hand_out",
    )(stream, update)


def solution(mesh):
    return jax.shard_map(
        per_device,
        mesh=mesh,
        in_specs=(
            P(("ctx", "mp"), None, None, None),
            P(("ctx", "mp"), None, None, None),
            P(("ctx", "mp"), None, None, None),
            P(),
            P("ctx", "mp"),
            P("ctx", "mp"),
            P("mp"),
            P("mp", "ctx"),
            P("mp", "ctx"),
            P("ctx", "mp"),
        ),
        out_specs=(P("ctx", "mp"), P("ctx", "mp")),
        check_vma=False,
    )
```

```python
import functools
import math

import jax
import jax.numpy as jnp
from jax import lax
from jax.experimental import pallas as pl
from jax.experimental.pallas import tpu as pltpu
from jax.sharding import PartitionSpec as P

NX, NY, NZ, NK = 4, 4, 8, 2
CTX = NY * NZ * NK
ROWS, HEADS, GROUP, WIDTH = 256, 8, 8, 128
KEYS, SLOTS = 2048, 64
MODEL, LOCAL, HALF, UNITS = 8192, 2048, 1024, 224
EPS = 1e-5
LOWEST = -1e30
SCALE = WIDTH**-0.5 * math.log2(math.e)
MESH = pl.DeviceIdType.MESH
VMEM_LIMIT = 56 * 1024 * 1024
F32, BF16 = jnp.float32, jnp.bfloat16


def place():
    c = lax.axis_index("ctx")
    x = lax.axis_index("mp")
    return c, x, c // (NZ * NK), (c // NK) % NZ, c % NK


def ctx_of(y, z, k):
    return (y * NZ + z) * NK + k


def remote(src, dst, send_sem, recv_sem, ctx, mp):
    return pltpu.make_async_remote_copy(
        src_ref=src,
        dst_ref=dst,
        send_sem=send_sem,
        recv_sem=recv_sem,
        device_id=(ctx, mp),
        device_id_type=MESH,
    )


def dot(a, b, da, db):
    return lax.dot_general(a, b, (((da,), (db,)), ((), ())), preferred_element_type=F32)


def hp_at(t, y):
    return ((y // 2 + t % 2) % 2) * 2 + (y % 2 + t // 2) % 2


def layer_kernel(
    own_hbm, chosen_hbm, residual_ref, gain_hbm, keys_ref, values_ref, wo_hbm, wg_hbm, wu_hbm, wd_hbm,
    stream_ref, update_ref,
    own_ref, chosen_ref, gain_ref, qbuf, qpair, kbuf, vbuf, q32, o32, st32, sendbuf, msg, tops_out, tops_in, picked, ranks, plane, slots_vmem, slots,
    wo, wg, wu, wd, weight, stats, running, num_t, xmsg, att_t,
    core_out, core_in, y_out, y_in, z_out, z_in,
    z_all, x_all, gu32, gu_out, gu_in, hid,
    k_sem, v_sem, s_sem,
    qz_send, qz_recv, p2_send, p2_recv, p3_send, p3_recv, p4_send, p4_recv, qc_send, qc_recv,
    a_send, a_recv, b_send, b_recv, i_sem,
    w_sem, x_send, x_recv,
    c_send, c_recv, y_send, y_recv, z_send, z_recv,
    gz_send, gz_recv, gy_send, gy_recv, gc_send, gc_recv,
    r_send, r_recv, h_send, h_recv,
):
    c, x, y, z, k = place()
    other = ctx_of(y, z, 1 - k)
    pending = []

    barrier = pltpu.get_barrier_semaphore()
    pl.semaphore_signal(barrier, inc=1, device_id=(other, x), device_id_type=MESH)
    for j in range(1, NX):
        pl.semaphore_signal(barrier, inc=1, device_id=(c, (x + j) % NX), device_id_type=MESH)
    for j in range(1, NY):
        pl.semaphore_signal(barrier, inc=1, device_id=(ctx_of((y + j) % NY, z, k), x), device_id_type=MESH)
    for j in range(1, NZ):
        pl.semaphore_signal(barrier, inc=1, device_id=(ctx_of(y, (z + j) % NZ, k), x), device_id_type=MESH)

    def load(t, carry):
        h = hp_at(t // 2, y) * 2 + t % 2
        pltpu.make_async_copy(keys_ref.at[h], kbuf.at[h], k_sem.at[h]).start()
        pltpu.make_async_copy(values_ref.at[h], vbuf.at[h], v_sem.at[h]).start()
        return carry

    row_a = ((k * NX + x) * NY + y) * NZ
    row_b = ((k * NY + y) * NX + x) * NZ
    given = [
        pltpu.make_async_copy(own_hbm, own_ref, i_sem.at[0]),
        pltpu.make_async_copy(chosen_hbm, chosen_ref, i_sem.at[1]),
        pltpu.make_async_copy(gain_hbm, gain_ref, i_sem.at[2]),
    ]
    for cp in given:
        cp.start()
    given[0].wait()
    qbuf[0:2, row_a + z] = own_ref[0:2]
    qbuf[2:4, row_b + z] = own_ref[2:4]
    pl.semaphore_wait(barrier, 1 + NX - 1 + NY - 1 + NZ - 1)

    arrivals = []
    for j in range(1, NZ):
        to = ctx_of(y, (z + j) % NZ, k)
        for half, row in ((0, row_a), (1, row_b)):
            ref = qbuf.at[pl.ds(2 * half, 2), row + z]
            cp = remote(ref, ref, qz_send.at[half, j - 1], qz_recv.at[half, j - 1], to, x)
            cp.start()
            arrivals.append(cp)
    pending += arrivals
    lax.fori_loop(0, HEADS, load, 0)

    loads = [
        pltpu.make_async_copy(wo_hbm, wo, w_sem.at[0]),
        pltpu.make_async_copy(wg_hbm, wg, w_sem.at[1]),
        pltpu.make_async_copy(wu_hbm, wu, w_sem.at[2]),
        pltpu.make_async_copy(wd_hbm, wd.at[pl.ds(0, UNITS)], w_sem.at[3]),
    ]
    for cp in loads:
        cp.start()
    wd[UNITS:256, :] = jnp.zeros((256 - UNITS, LOCAL), BF16)

    for cp in given[1:]:
        cp.wait()

    r_in = lax.broadcasted_iota(jnp.int32, (ROWS, ROWS), 0)
    r_out = lax.broadcasted_iota(jnp.int32, (ROWS, ROWS), 1)
    moved = ((r_in // 64) * 32 + ((r_in // 8) % 8) * 4 + r_in % 4) + ((r_in // 4) % 2) * 128
    permute = jnp.where(moved == r_out, 1.0, 0.0).astype(BF16)
    before = jnp.where(r_in < r_out, 1.0, 0.0).astype(BF16)
    listed = chosen_ref[...].reshape(HEADS * 16, ROWS).astype(F32).astype(BF16)
    picked[...] = dot(listed, permute, 1, 0)
    own_id = (c * NX + x).astype(F32)
    found = [
        jnp.max(jnp.where(picked[h * 16 : h * 16 + 16, :] == own_id, 1.0, 0.0), axis=0, keepdims=True)
        for h in range(HEADS)
    ]
    member = jnp.concatenate(found, axis=0)
    ranks[...] = jnp.where(member > 0.5, dot(jnp.concatenate([member, member], axis=0).astype(BF16), before, 1, 0)[0:HEADS], -1.0)
    ids = (lax.broadcasted_iota(jnp.int32, (CTX, ROWS), 0) * NX + x).astype(F32)
    member = jnp.zeros((CTX, ROWS), F32)
    for i in range(16):
        row = picked[pl.ds((c // GROUP) * 16 + i, 1), :]
        member = jnp.maximum(member, jnp.where(row == ids, 1.0, 0.0))
    plane[...] = jnp.where(member > 0.5, dot(member.astype(BF16), before, 1, 0), -1.0)
    r8 = lax.broadcasted_iota(jnp.int32, (16, ROWS), 1)
    kk, yy, zz, mm = r8 // 128, (r8 // 32) % 4, (r8 // 4) % 8, r8 % 4
    pos_a = (((kk * NX + mm) * NY + yy) * NZ + zz).astype(F32).astype(BF16)
    pos_b = (((kk * NY + yy) * NX + mm) * NZ + zz).astype(F32).astype(BF16)
    spot = lax.broadcasted_iota(jnp.int32, (128, ROWS), 0).astype(F32)
    for h in range(HEADS):
        hit = jnp.where(spot == ranks[h : h + 1, :], 1.0, 0.0).astype(BF16)
        at = dot(pos_a if h < 4 else pos_b, hit, 1, 1)
        slots_vmem[h : h + 1, :] = at[0:1].astype(jnp.int32)
    to_scalar = pltpu.make_async_copy(slots_vmem, slots, s_sem)
    to_scalar.start()
    for cp in arrivals:
        cp.wait_recv()

    arrivals = []
    for j in range(1, 4):
        ref = qbuf.at[0:2, pl.ds(row_a, NZ)]
        cp = remote(ref, ref, p2_send.at[0, j - 1], p2_recv.at[0, j - 1], ctx_of((y + j) % NY, z, k), x)
        cp.start()
        arrivals.append(cp)
        ref = qbuf.at[2:4, pl.ds(row_b, NZ)]
        cp = remote(ref, ref, p2_send.at[1, j - 1], p2_recv.at[1, j - 1], c, (x + j) % NX)
        cp.start()
        arrivals.append(cp)
    pending += arrivals

    def block(hp, n):
        return qbuf.at[hp, pl.ds(n * 32, 32)]

    def pass_on(hp, n, j):
        return remote(block(hp, n), block(hp, n), qc_send.at[hp, j], qc_recv.at[hp, j], other, x)

    def piece_of(hp, row, i, j):
        ref = qbuf.at[hp, pl.ds(row, NZ)]
        return ref, p4_send.at[hp, j - 1, i], p4_recv.at[hp, j - 1, i]

    for i in range(4):
        if i:
            for cp in arrivals[2 * i - 2 : 2 * i]:
                cp.wait_recv()
        for j in range(1, 4):
            ref, send, recv = piece_of(y % 2, ((k * NX + x) * NY + (y - i + NY) % NY) * NZ, i, j)
            remote(ref, ref, send, recv, c, (x + j) % NX).start()
            to = (y + j) % NY
            ref, send, recv = piece_of(2 + to % 2, ((k * NY + y) * NX + (x - i + NX) % NX) * NZ, i, j)
            remote(ref, ref, send, recv, ctx_of(to, z, k), x).start()
    for j in range(1, 4):
        hp = (y % 2 + 1) % 2
        ref = block(hp, k * NX + x)
        remote(ref, ref, p3_send.at[hp, j - 1], p3_recv.at[hp, j - 1], c, (x + j) % NX).start()
        to = (y + j) % NY
        hp = 2 + (to % 2 + 1) % 2
        ref = block(hp, k * NY + y)
        remote(ref, ref, p3_send.at[hp, j - 1], p3_recv.at[hp, j - 1], ctx_of(to, z, k), x).start()
    for hp in range(4):
        pass_on(hp, k * 4 + (x if hp < 2 else y), 0).start()

    def forward(hp, pieces):
        late = hp // 2
        for j in range(1, 4):
            n = k * 4 + (x * (1 - late) + y * late - j + 4) % 4
            ref = block(hp, n)
            if pieces:
                for i in range(4):
                    src, send, recv = piece_of(hp, n * 32, i, j)
                    remote(src, src, send, recv, other, x).wait_recv()
            else:
                remote(ref, ref, p3_send.at[hp, j - 1], p3_recv.at[hp, j - 1], other, x).wait_recv()
            pass_on(hp, n, j).start()

    forward(hp_at(0, y), True)
    forward(hp_at(1, y), True)
    to_scalar.wait()
    slot_iota = lax.broadcasted_iota(jnp.int32, (SLOTS, ROWS), 0).astype(F32)

    def head(h):
        hp = h // 2
        upper = (h % 2) == 1
        pltpu.make_async_copy(keys_ref.at[h], kbuf.at[h], k_sem.at[h]).wait()
        pltpu.make_async_copy(values_ref.at[h], vbuf.at[h], v_sem.at[h]).wait()

        def pick(i, carry):
            for u in range(8):
                s = i * 8 + u
                row = jnp.minimum(jnp.maximum(slots[h, s], 0), ROWS - 1)
                tile = qpair[row].astype(F32)
                q32[pl.ds(pl.multiple_of(s * 8, 8), 8), :] = jnp.where(upper, tile[8:16], tile[0:8])
            return carry

        lax.fori_loop(0, SLOTS // 8, pick, 0)

        for b in range(1):
            at = pl.ds(b * 512, 512)
            s = dot(q32[at, :].astype(BF16), kbuf[h], 1, 1)
            top = (jnp.max(s, axis=1, keepdims=True) * SCALE).astype(BF16).astype(F32)
            p = jnp.exp2(s * SCALE - top)
            total = jnp.sum(p, axis=1, keepdims=True)
            o32[at, :] = dot(p.astype(BF16), vbuf[h], 1, 0)
            lane = lax.broadcasted_iota(jnp.int32, (512, WIDTH), 1)
            st32[at, :] = jnp.where(lane == 0, top, total)

        lane = lax.broadcasted_iota(jnp.int32, (SLOTS, WIDTH), 1)
        slot = lax.broadcasted_iota(jnp.int32, (SLOTS, WIDTH), 0)
        for g in range(GROUP):
            n = h * GROUP + g
            sendbuf[n] = o32[pl.ds(g, SLOTS, stride=GROUP), :].astype(BF16)
            st = st32[pl.ds(g, SLOTS, stride=GROUP), :]
            spread = jnp.where(lane == slot, st[:, 0:1], jnp.where(lane == slot + SLOTS, st[:, 1:2], 0.0))
            tops_out[n] = jnp.sum(spread, axis=0, keepdims=True)

            @pl.when(n != c)
            def _():
                remote(sendbuf.at[n], msg.at[c], a_send.at[n], a_recv.at[c], n, x).start()
                remote(tops_out.at[n], tops_in.at[c], b_send.at[n], b_recv.at[c], n, x).start()

            @pl.when(n == c)
            def _():
                msg[c] = sendbuf[n]
                tops_in[c] = tops_out[n]

    def pair(t, carry):
        hp = hp_at(t, y)
        for j in range(4):
            pass_on(hp, 0, j).wait_recv()
        qpair[...] = qbuf[hp]
        lax.fori_loop(0, 2, lambda i, v: (head(hp * 2 + i), v)[1], 0)

        @pl.when(t < 2)
        def _():
            forward(hp_at(t + 2, y), False)

        return carry

    lax.fori_loop(0, 4, pair, 0)

    num_t[...] = jnp.zeros_like(num_t)
    running[0:1, :] = jnp.full((1, ROWS), LOWEST, F32)
    running[1:2, :] = jnp.zeros((1, ROWS), F32)

    def merge(t, carry):
        base = hp_at(t, y) * (NZ * NK)

        def arrive(i, v):
            s = base + i

            @pl.when(s != c)
            def _():
                remote(sendbuf.at[s], msg.at[s], a_send.at[s], a_recv.at[s], s, x).wait_recv()
                remote(tops_out.at[s], tops_in.at[s], b_send.at[s], b_recv.at[s], s, x).wait_recv()

            return v

        lax.fori_loop(0, NZ * NK, arrive, 0)
        for i in range(NZ * NK):
            stats[i : i + 1, :] = tops_in[base + i]
        held = stats[...]
        rank = plane[pl.ds(pl.multiple_of(base, 16), 16), :]
        at = jnp.maximum(rank, 0.0).astype(jnp.int32)

        def by_row(first):
            return jnp.concatenate(
                [
                    jnp.take_along_axis(held, at[:, i * 128 : (i + 1) * 128] + first, axis=1, mode="promise_in_bounds")
                    for i in range(2)
                ],
                axis=1,
            )

        listed = rank >= 0.0
        top_each = jnp.where(listed, by_row(0), LOWEST)
        old = running[0:1, :]
        top = jnp.maximum(old, jnp.max(top_each, axis=0, keepdims=True))
        keep = jnp.exp2(old - top)
        w = jnp.where(listed, jnp.exp2(top_each - top), 0.0).astype(BF16).astype(F32)
        running[0:1, :] = top
        running[1:2, :] = running[1:2, :] * keep + jnp.sum(w * by_row(SLOTS), axis=0, keepdims=True)
        total = num_t[...] * keep
        for i in range(NZ * NK // 4):
            for u in range(4):
                s = i * 4 + u
                weight[s * SLOTS : (s + 1) * SLOTS, :] = jnp.where(
                    slot_iota == rank[s : s + 1, :], w[s : s + 1, :], 0.0
                ).astype(BF16)
            values = jnp.concatenate([msg[base + i * 4 + u] for u in range(4)], axis=0)
            total = total + dot(values, weight[i * 4 * SLOTS : (i + 1) * 4 * SLOTS, :], 0, 0)
        num_t[...] = total
        return carry

    lax.fori_loop(0, 4, merge, 0)

    top, den = running[0:1, :], running[1:2, :]

    xmsg[x, 0:WIDTH, :] = num_t[...].astype(BF16)
    den_high = den.astype(BF16).astype(F32)
    xmsg[x, WIDTH : WIDTH + 16, :] = jnp.concatenate(
        [top, den_high, den - den_high, jnp.zeros((13, ROWS), F32)], axis=0
    ).astype(BF16)
    arrivals = []
    for j in range(1, NX):
        cp = remote(xmsg.at[x], xmsg.at[x], x_send.at[j - 1], x_recv.at[j - 1], c, (x + j) % NX)
        cp.start()
        arrivals.append(cp)
    pending += arrivals
    for cp in arrivals:
        cp.wait_recv()
    tails = [xmsg[i, WIDTH : WIDTH + 16, :].astype(F32) for i in range(NX)]
    best = functools.reduce(jnp.maximum, [v[0:1] for v in tails])
    num, den = 0.0, 0.0
    for i in range(NX):
        f = jnp.exp2(tails[i][0:1] - best)
        den = den + f * (tails[i][1:2] + tails[i][2:3])
        num = num + f * xmsg[i, 0:WIDTH, :].astype(F32)
    att_t[...] = (num / den).astype(BF16)

    def half(v_ref, which):
        return v_ref[:, pl.ds(pl.multiple_of(which * 128, 128), 128)]

    def reduce_scatter(n, piece, use):
        cores, along_y, along_z = [], [], []
        for h in range(2):
            core_out[n, h] = piece(1 - k, h).astype(BF16)
            cp = remote(core_out.at[n, h], core_in.at[n, h], c_send.at[n, h], c_recv.at[n, h], other, x)
            cp.start()
            cores.append(cp)
        for h in range(2):
            mine = piece(k, h)
            cores[h].wait_recv()
            total = mine + core_in[n, h].astype(F32)
            y_out[n, h] = total.reshape(NY, 32, HALF).astype(BF16)
            copies = []
            for j in range(1, NY):
                to = (y + j) % NY
                cp = remote(
                    y_out.at[n, h, to], y_in.at[n, h, j - 1], y_send.at[n, h, j - 1], y_recv.at[n, h, j - 1], ctx_of(to, z, k), x
                )
                cp.start()
                copies.append(cp)
            along_y.append(copies)
        for h in range(2):
            acc = y_out[n, h, y].astype(F32)
            for j, cp in enumerate(along_y[h]):
                cp.wait_recv()
                acc = acc + y_in[n, h, j].astype(F32)
            regroup(acc, z_out.at[n, h])
            copies = []
            for j in range(1, NZ):
                to = (z + j) % NZ
                cp = remote(
                    z_out.at[n, h, to], z_in.at[n, h, j - 1], z_send.at[n, h, j - 1], z_recv.at[n, h, j - 1], ctx_of(y, to, k), x
                )
                cp.start()
                copies.append(cp)
            along_z.append(copies)
        for h in range(2):
            acc = z_out[n, h, z].astype(F32)
            for j, cp in enumerate(along_z[h]):
                cp.wait_recv()
                acc = acc + z_in[n, h, j].astype(F32)
            use(h, acc)
        for copies in [cores] + along_y + along_z:
            pending.extend(copies)

    rows_z, rows_y, rows_c = [], [], []

    def spread(h, projected):
        stream = (fold(residual_ref[:, h * HALF : (h + 1) * HALF].astype(F32)) + projected).astype(BF16)
        z_all[h, z] = stream
        for j in range(1, NZ):
            cp = remote(z_all.at[h, z], z_all.at[h, z], gz_send.at[h, j - 1], gz_recv.at[h, j - 1], ctx_of(y, (z + j) % NZ, k), x)
            cp.start()
            rows_z.append(cp)
        unfold(stream.astype(F32), stream_ref, h)

    loads[0].wait()
    reduce_scatter(0, lambda which, h: dot(half(att_t, which), wo[:, h * HALF : (h + 1) * HALF], 0, 0), spread)
    for h in range(2):
        for cp in rows_z[h * (NZ - 1) : (h + 1) * (NZ - 1)]:
            cp.wait_recv()

        def put(b, v):
            x_all[h, k, y, :, b * 256 : (b + 1) * 256] = v

        ungroup(z_all.at[h], put)
        for j in range(1, NY):
            ref = x_all.at[h, k, y]
            cp = remote(ref, ref, gy_send.at[h, j - 1], gy_recv.at[h, j - 1], ctx_of((y + j) % NY, z, k), x)
            cp.start()
            rows_y.append(cp)

    def gate_up(which, h):
        wide = x_all[h, which].reshape(128, HALF).astype(F32)
        squares = jnp.sum(wide * wide, axis=1, keepdims=True)
        cut = slice(h * HALF, (h + 1) * HALF)
        scaled = (wide * gain_ref[:, cut]).astype(BF16)
        lane = lax.broadcasted_iota(jnp.int32, (128, 256 - UNITS), 1)
        parts = [dot(scaled, weight_ref[:, cut], 1, 1) for weight_ref in (wg, wu)]
        if h == 0:
            for n in range(2):
                gu32[n, which, :, 0:UNITS] = parts[n]
            gu32[0, which, :, UNITS:256] = jnp.where(lane < 2, squares, 0.0)
            gu32[1, which, :, UNITS:256] = jnp.zeros((128, 256 - UNITS), F32)
        else:
            for n in range(2):
                gu32[n, which, :, 0:UNITS] += parts[n]
            squares = squares + gu32[0, which, :, UNITS : UNITS + 1]
            high = squares.astype(BF16).astype(F32)
            gu32[0, which, :, UNITS:256] = jnp.where(lane == 0, high, squares - high)

    loads[1].wait()
    loads[2].wait()
    for h in range(2):
        for cp in rows_y[h * (NY - 1) : (h + 1) * (NY - 1)]:
            cp.wait_recv()
        cp = remote(x_all.at[h, k], x_all.at[h, k], gc_send.at[h], gc_recv.at[h], other, x)
        cp.start()
        rows_c.append(cp)
        gate_up(k, h)
    for h in range(2):
        rows_c[h].wait_recv()
        gate_up(1 - k, h)
    pending += rows_z + rows_y + rows_c

    for q in range(NX):
        for n in range(2):
            gu_out[q, n] = gu32[n, q // 2, (q % 2) * 64 : (q % 2) * 64 + 64, :].astype(BF16)
    arrivals = []
    for j in range(1, NX):
        to = (x + j) % NX
        cp = remote(gu_out.at[to], gu_in.at[j - 1], r_send.at[j - 1], r_recv.at[j - 1], c, to)
        cp.start()
        pending.append(cp)
        arrivals.append(cp)
    acc = gu_out[x].astype(F32)
    for j, cp in enumerate(arrivals):
        cp.wait_recv()
        acc = acc + gu_in[j].astype(F32)
    squares = acc[0, :, UNITS : UNITS + 1] + acc[0, :, UNITS + 1 : UNITS + 2]
    factor = lax.rsqrt(squares / MODEL + EPS)
    gate = acc[0] * factor
    up = acc[1] * factor
    lane = lax.broadcasted_iota(jnp.int32, (64, 256), 1)
    hidden = jnp.where(lane < UNITS, gate / (1.0 + jnp.exp(-gate)) * up, 0.0)
    hid[x] = hidden.astype(BF16)
    arrivals = []
    for j in range(1, NX):
        cp = remote(hid.at[x], hid.at[x], h_send.at[j - 1], h_recv.at[j - 1], c, (x + j) % NX)
        cp.start()
        pending.append(cp)
        arrivals.append(cp)
    for cp in arrivals:
        cp.wait_recv()
    loads[3].wait()

    def down(which, h):
        rows = hid[pl.ds(which * 2, 2)].reshape(128, 256)
        return dot(rows, wd[:, h * HALF : (h + 1) * HALF], 1, 0)

    reduce_scatter(1, down, lambda h, total: unfold(total, update_ref, h))
    for cp in pending:
        cp.wait_send()
    for j in range(1, 4):
        to = (y + j) % NY
        for first in (y % 2, 2 + to % 2):
            for i in range(4):
                src, send, recv = piece_of(first, 0, i, j)
                remote(src, src, send, recv, other, x).wait_send()
        for hp in ((y % 2 + 1) % 2, 2 + (to % 2 + 1) % 2):
            remote(block(hp, 0), block(hp, 0), p3_send.at[hp, j - 1], p3_recv.at[hp, j - 1], other, x).wait_send()
    for hp in range(4):
        for j in range(4):
            pass_on(hp, 0, j).wait_send()

    def sent(n, carry):
        @pl.when(n != c)
        def _():
            remote(sendbuf.at[n], msg.at[n], a_send.at[n], a_recv.at[n], n, x).wait_send()
            remote(tops_out.at[n], tops_in.at[n], b_send.at[n], b_recv.at[n], n, x).wait_send()

        return carry

    lax.fori_loop(0, CTX, sent, 0)

def swap4(v):
    return pltpu.roll(v, 4, 1)


def fold(v):
    return jnp.concatenate([v[:, b * 256 : (b + 1) * 256] for b in range(4)], axis=0)


def unfold(v, out_ref, h):
    for b in range(4):
        at = h * HALF + b * 256
        out_ref[:, at : at + 256] = v[4 * b : 4 * b + 4].astype(BF16)


def regroup(acc, out_ref):
    parts = [acc[:, b * 256 : (b + 1) * 256].reshape(4, 8, 256) for b in range(4)]
    lower = lax.broadcasted_iota(jnp.int32, (4, 8, 256), 1) < 4
    even = [jnp.where(lower, parts[b], swap4(parts[b + 1])) for b in (0, 2)]
    odd = [jnp.where(lower, swap4(parts[b]), parts[b + 1]) for b in (0, 2)]
    for t in range(4):
        out_ref[2 * t] = jnp.concatenate([even[0][t], even[1][t]], axis=0).astype(BF16)
        out_ref[2 * t + 1] = jnp.concatenate([odd[0][t], odd[1][t]], axis=0).astype(BF16)


def ungroup(src_ref, store):
    a = src_ref[...].astype(F32)
    lower = lax.broadcasted_iota(jnp.int32, (8, 256), 0) < 4
    columns = [[], [], [], []]
    for t in range(4):
        for q in range(2):
            e = a[2 * t, 8 * q : 8 * q + 8]
            o = a[2 * t + 1, 8 * q : 8 * q + 8]
            columns[2 * q].append(jnp.where(lower, e, pltpu.roll(o, 4, 0)))
            columns[2 * q + 1].append(jnp.where(lower, pltpu.roll(e, 4, 0), o))
    for b in range(4):
        store(b, jnp.concatenate(columns[b], axis=0).astype(BF16))


def hand_out(stream_in, update_in, stream_ref, update_ref):
    stream_ref[...] = stream_in[...]
    update_ref[...] = update_in[...]


def dma(*shape):
    return pltpu.SemaphoreType.DMA(shape)


def per_device(query, keys, values, chosen, residual, output_weight, norm_gain, gate_weight, up_weight, down_weight):
    vmem = pl.BlockSpec(memory_space=pltpu.VMEM)
    hbm = pl.BlockSpec(memory_space=pl.ANY)
    stream, update = pl.pallas_call(
        layer_kernel,
        out_shape=[jax.ShapeDtypeStruct((4, LOCAL), BF16)] * 2,
        in_specs=[hbm, hbm, vmem, hbm, hbm, hbm, hbm, hbm, hbm, hbm],
        out_specs=[vmem, vmem],
        scratch_shapes=[
            pltpu.VMEM((4, 16, WIDTH), BF16),
            pltpu.VMEM((HEADS, 16, ROWS), jnp.int32),
            pltpu.VMEM((1, LOCAL), F32),
            pltpu.VMEM((4, ROWS, 16, WIDTH), BF16),
            pltpu.VMEM((ROWS, 16, WIDTH), BF16),
            pltpu.VMEM((HEADS, KEYS, WIDTH), BF16),
            pltpu.VMEM((HEADS, KEYS, WIDTH), BF16),
            pltpu.VMEM((SLOTS * GROUP, WIDTH), F32),
            pltpu.VMEM((SLOTS * GROUP, WIDTH), F32),
            pltpu.VMEM((SLOTS * GROUP, WIDTH), F32),
            pltpu.VMEM((CTX, SLOTS, WIDTH), BF16),
            pltpu.VMEM((CTX, SLOTS, WIDTH), BF16),
            pltpu.VMEM((CTX, 1, WIDTH), F32),
            pltpu.VMEM((CTX, 1, WIDTH), F32),
            pltpu.VMEM((HEADS * 16, ROWS), F32),
            pltpu.VMEM((HEADS, ROWS), F32),
            pltpu.VMEM((CTX, ROWS), F32),
            pltpu.VMEM((HEADS, 128), jnp.int32),
            pltpu.SMEM((HEADS, 128), jnp.int32),
            pltpu.VMEM((WIDTH, LOCAL), BF16),
            pltpu.VMEM((UNITS, LOCAL), BF16),
            pltpu.VMEM((UNITS, LOCAL), BF16),
            pltpu.VMEM((256, LOCAL), BF16),
            pltpu.VMEM((16 * SLOTS, ROWS), BF16),
            pltpu.VMEM((16, WIDTH), F32),
            pltpu.VMEM((8, ROWS), F32),
            pltpu.VMEM((WIDTH, ROWS), F32),
            pltpu.VMEM((NX, WIDTH + 16, ROWS), BF16),
            pltpu.VMEM((WIDTH, ROWS), BF16),
            pltpu.VMEM((2, 2, 128, HALF), BF16),
            pltpu.VMEM((2, 2, 128, HALF), BF16),
            pltpu.VMEM((2, 2, NY, 32, HALF), BF16),
            pltpu.VMEM((2, 2, NY - 1, 32, HALF), BF16),
            pltpu.VMEM((2, 2, NZ, 16, 256), BF16),
            pltpu.VMEM((2, 2, NZ - 1, 16, 256), BF16),
            pltpu.VMEM((2, NZ, 16, 256), BF16),
            pltpu.VMEM((2, NK, NY, 32, HALF), BF16),
            pltpu.VMEM((2, NK, 128, 256), F32),
            pltpu.VMEM((NX, 2, 64, 256), BF16),
            pltpu.VMEM((NX - 1, 2, 64, 256), BF16),
            pltpu.VMEM((NX, 64, 256), BF16),
            dma(HEADS), dma(HEADS), pltpu.SemaphoreType.DMA,
            dma(2, 7), dma(2, 7), dma(2, 3), dma(2, 3), dma(4, 3), dma(4, 3), dma(4, 3, 4), dma(4, 3, 4), dma(4, 4), dma(4, 4),
            dma(CTX), dma(CTX), dma(CTX), dma(CTX), dma(3),
            dma(4), dma(3), dma(3),
            dma(2, 2), dma(2, 2), dma(2, 2, 3), dma(2, 2, 3), dma(2, 2, 7), dma(2, 2, 7),
            dma(2, 7), dma(2, 7), dma(2, 3), dma(2, 3), dma(2), dma(2),
            dma(3), dma(3), dma(3), dma(3),
        ],
        compiler_params=pltpu.CompilerParams(collective_id=0, has_side_effects=True, vmem_limit_bytes=VMEM_LIMIT),
        name="layer",
    )(
        query.reshape(4, 16, WIDTH), chosen.transpose(0, 2, 1), residual, norm_gain.reshape(1, LOCAL),
        keys[0], values[0], output_weight, gate_weight.T, up_weight.T, down_weight,
    )
    return pl.pallas_call(
        hand_out,
        out_shape=[jax.ShapeDtypeStruct((4, LOCAL), BF16)] * 2,
        in_specs=[vmem, vmem],
        out_specs=[vmem, vmem],
        name="hand_out",
    )(stream, update)


def solution(mesh):
    return jax.shard_map(
        per_device,
        mesh=mesh,
        in_specs=(
            P(("ctx", "mp"), None, None, None),
            P(("ctx", "mp"), None, None, None),
            P(("ctx", "mp"), None, None, None),
            P(),
            P("ctx", "mp"),
            P("ctx", "mp"),
            P("mp"),
            P("mp", "ctx"),
            P("mp", "ctx"),
            P("ctx", "mp"),
        ),
        out_specs=(P("ctx", "mp"), P("ctx", "mp")),
        check_vma=False,
    )
```
